768 devices in a mesh: blk: 96 (over z_hi, x, y), grp: 8 (over z_lo, core).
Axes of the slice: x: 4, y: 8, z: 12 (z_hi: 3, z_lo: 4; z = z_hi * 4 + z_lo), core: 2. Of those that a mesh axis runs over, the one named last changes fastest.
Arguments:
- frequency_features: bfloat16 [98304, 1024], P(('blk', 'grp')), may hold values from -0.1875 to 0.1875
- sentence_features: bfloat16 [98304, 1024], P(('blk', 'grp')), may hold values from -0.1875 to 0.1875
- score_multiplier: float32 [1], replicated, may hold values from 4 to 20
- score_offset_term: float32 [1], replicated, may hold values from -4 to -1
Outputs:
- picture_derivatives: bfloat16 [98304, 1024], P(('blk', 'grp'))
- sentence_derivatives: bfloat16 [98304, 1024], P(('blk', 'grp'))
The draws below stay inside these ranges and needn't reach their ends.
All inputs are finite; a program needn't handle non-finite values.
Results may differ from the reference program's by a relative error of at most 0.012.
Values may be sent and summed in bfloat16 or wider, within the bound.
No kernel may reach another device: no remote copies, remote signals or barrier semaphores. Data moves between devices by JAX's collectives and lax.ppermute only.
A program may use at most 32 MiB of HBM per device.

```python
import math
import jax
import jax.numpy as jnp
from jax import lax

FEATURE_WIDTH = 1024
ROWS = 128
HOPS = 1
PAIR_TOTAL = 98304
N_BLK = 96
N_GRP = 8


def levels(own_key, shape, pieces, least, high):
    loudness = 1.0
    for position, parts in pieces:
        heights = jax.random.uniform(jax.random.fold_in(jax.random.fold_in(own_key, 6), position), (parts,), jnp.float32, least / len(pieces), high / len(pieces))
        loudness = loudness * jnp.repeat(jnp.exp(heights), shape[position] // parts).reshape((-1,) + (1,) * (len(shape) - 1 - position))
    return loudness


def normal_values(stream_key, extent, scale, limit, cuts=(), kind=jnp.bfloat16):
    array = scale * jax.random.normal(stream_key, extent, jnp.float32)
    if cuts:
        array = array * levels(stream_key, extent, cuts, -0.22, 0.18)
    return jnp.clip(array, -limit, limit).astype(kind)


def setup_inputs(seed: int = 0) -> dict:
    key_of = jax.random.split(jax.random.key(seed), 5)
    return {
        "frequency_features": normal_values(key_of[0], (PAIR_TOTAL, FEATURE_WIDTH), FEATURE_WIDTH ** -0.5, 0.1875, ((0, 768),)),
        "sentence_features": normal_values(key_of[1], (PAIR_TOTAL, FEATURE_WIDTH), FEATURE_WIDTH ** -0.5, 0.1875, ((0, 768),)),
        "score_multiplier": jnp.clip(jnp.exp(jax.random.uniform(key_of[2], (1,), jnp.float32, math.log(4.0), math.log(20.0))), 4.0, 20.0),
        "score_offset_term": jnp.clip(jax.random.uniform(key_of[3], (1,), jnp.float32, -4.0, -1.0), -4.0, -1.0),
    }


def reference(frequency_features, sentence_features, score_multiplier, score_offset_term):
    block_rows = N_GRP * ROWS
    image_blocks = frequency_features.reshape(N_BLK, block_rows, FEATURE_WIDTH).astype(jnp.float32)
    text_blocks = sentence_features.reshape(N_BLK, block_rows, FEATURE_WIDTH).astype(jnp.float32)
    reciprocal_warmth = score_multiplier[0]
    tile_stride_amount = score_offset_term[0]
    diagonal = jnp.eye(block_rows, dtype=bool)
    picture_count = jnp.zeros((N_BLK, block_rows, FEATURE_WIDTH), jnp.float32)
    sentence_count = jnp.zeros((N_BLK, block_rows, FEATURE_WIDTH), jnp.float32)
    for offset in range(0, HOPS + 1):
        counterpart_device = jnp.roll(text_blocks, -offset, axis=0)
        if offset == 0:
            labels = jnp.where(diagonal, 1.0, -1.0).astype(jnp.float32)
        else:
            labels = jnp.full((block_rows, block_rows), -1.0, jnp.float32)

        def one_block(pair):
            picture_matrix, sentence_matrix = pair
            pair_scores = jnp.einsum("fh,wh->fw", picture_matrix, sentence_matrix) * reciprocal_warmth + tile_stride_amount
            slopes = (-labels * jax.nn.sigmoid(-labels * pair_scores)).astype(jnp.bfloat16)
            slopes = lax.optimization_barrier(slopes).astype(jnp.float32)
            image_part = jnp.einsum("ij,jd->id", slopes, sentence_matrix)
            window_slope_slices = slopes.reshape(N_GRP, ROWS, block_rows)
            sliced_images = picture_matrix.reshape(N_GRP, ROWS, FEATURE_WIDTH)
            terms = jnp.einsum("gij,gid->gjd", window_slope_slices, sliced_images).astype(jnp.bfloat16)
            terms = lax.optimization_barrier(terms).astype(jnp.float32)
            return image_part, jnp.sum(terms, axis=0)

        image_part, text_part = lax.map(one_block, (image_blocks, counterpart_device))
        picture_count = picture_count + image_part
        sentence_count = sentence_count + jnp.roll(text_part, offset, axis=0)
    picture_derivatives = (reciprocal_warmth * picture_count).astype(jnp.bfloat16).reshape(PAIR_TOTAL, FEATURE_WIDTH)
    sentence_derivatives = (reciprocal_warmth * sentence_count).astype(jnp.bfloat16).reshape(PAIR_TOTAL, FEATURE_WIDTH)
    return (picture_derivatives, sentence_derivatives)
```

```python
import jax
import jax.numpy as jnp
from jax import lax
from jax.sharding import Mesh, PartitionSpec as P

CHIPS = 4
CORES = 2


def moved(array, axes, pairs):
    return lax.ppermute(array, axes, pairs)


def body(images, captions, multiplier, offset):
    scale = multiplier[0]
    bias = offset[0]
    rows = images.shape[0]
    blocks = lax.axis_size("blk")
    chip = lax.axis_index("zl")
    low = chip < 2
    inner = jnp.logical_or(chip == 1, chip == 2)

    own = jnp.where(low, captions, images)
    other = jnp.where(low, images, captions)
    both = jnp.concatenate([own, other])

    from_end = moved(both, "zl", [(0, 1), (3, 2)])
    from_inner = moved(both, "zl", [(1, 2), (2, 1)])
    from_far_end = moved(both, "zl", [(0, 2), (3, 1)])

    def neighbour(array, low_source, high_source):
        pairs = []
        for p in range(blocks):
            pairs.append((((p + 1) % blocks) * CHIPS + low_source, p * CHIPS + 1))
            pairs.append((((p - 1) % blocks) * CHIPS + high_source, p * CHIPS + 2))
        return moved(array, ("blk", "zl"), pairs)

    near = [
        neighbour(own, 1, 2),
        neighbour(own, 0, 3),
        neighbour(other, 2, 1),
        neighbour(other, 3, 0),
    ]

    left = jnp.concatenate([other, from_end[rows:], from_inner[:rows], from_far_end[:rows]])
    right = jnp.concatenate([own, from_end[:rows], from_inner[rows:], from_far_end[rows:]])
    next_right = jnp.concatenate(near)
    swap = [(0, 1), (1, 0)]
    right = jnp.concatenate([right, moved(right, "core", swap)])
    next_right = jnp.concatenate([next_right, moved(next_right, "core", swap)])

    def slopes_of(columns, paired):
        scores = lax.dot_general(
            left, columns, (((1,), (1,)), ((), ())), preferred_element_type=jnp.float32
        )
        scores = scores * scale + bias
        slopes = jax.nn.sigmoid(scores)
        if paired:
            row = lax.broadcasted_iota(jnp.int32, slopes.shape, 0)
            column = lax.broadcasted_iota(jnp.int32, slopes.shape, 1)
            slopes = jnp.where(row == column, -jax.nn.sigmoid(-scores), slopes)
        return slopes.astype(jnp.bfloat16)

    total = jnp.dot(slopes_of(right, True), right, preferred_element_type=jnp.float32)
    total = total + jnp.dot(slopes_of(next_right, False), next_right, preferred_element_type=jnp.float32)
    result = (scale * total).astype(jnp.bfloat16)

    to_end = moved(result[rows : 2 * rows], "zl", [(1, 0), (2, 3)])
    to_inner = moved(result[2 * rows : 3 * rows], "zl", [(1, 2), (2, 1)])
    to_far_end = moved(result[3 * rows :], "zl", [(1, 3), (2, 0)])
    own_result = jnp.where(inner, result[:rows], to_end)
    other_result = jnp.where(inner, to_inner, to_far_end)
    return (jnp.where(low, own_result, other_result), jnp.where(low, other_result, own_result))


def solution(mesh):
    fine = Mesh(mesh.devices.reshape(-1, CHIPS, CORES), ("blk", "zl", "core"))
    rows = P(("blk", "zl", "core"), None)
    return jax.shard_map(
        body, mesh=fine, in_specs=(rows, rows, P(), P()), out_specs=(rows, rows), check_vma=False
    )
```

```python
import functools
import math

import jax
import jax.numpy as jnp
from jax import lax
from jax.experimental import pallas as pl
from jax.experimental.pallas import tpu as pltpu
from jax.sharding import Mesh, PartitionSpec as P

CHIPS = 4
CORES = 2
LIMIT = 16 * 1024 * 1024


def in_vmem(kernel, shapes, *operands, flops=0, scalars=0, scratch=()):
    moved_bytes = sum(math.prod(s.shape) * s.dtype.itemsize for s in shapes)
    return pl.pallas_call(
        kernel,
        out_shape=shapes,
        in_specs=[pl.BlockSpec(memory_space=pltpu.SMEM)] * scalars
        + [pl.BlockSpec(memory_space=pltpu.VMEM)] * (len(operands) - scalars),
        out_specs=[pl.BlockSpec(memory_space=pltpu.VMEM)] * len(shapes),
        scratch_shapes=[pltpu.VMEM(s.shape, s.dtype) for s in scratch],
        compiler_params=pltpu.CompilerParams(vmem_limit_bytes=LIMIT),
        cost_estimate=pl.CostEstimate(flops=flops, bytes_accessed=moved_bytes, transcendentals=0),
    )(*operands)


def pack_kernel(rows, own, other, own_far, xe, xo, y0, af, to_near, to_last, w1, left, first):
    gathered(to_near, [(xe, 0, rows), (xo, 1, rows)])
    gathered(to_last, [(other, 0, rows), (y0, 0, rows)])
    gathered(w1, [(xe, 0, rows), (xo, 1, rows), (y0, 0, rows)])
    gathered(left, [(other, 0, rows), (xe, 1, rows), (xo, 0, rows), (af, 0, rows)])
    gathered(first, [(own, 0, rows), (own_far, 0, rows)])


def slopes_of(scores, scale, bias, diagonal=None):
    scores = scores * scale + bias
    if diagonal is not None:
        scores = jnp.where(diagonal, -scores, scores)
    slopes = 1.0 / (1.0 + jnp.exp(-scores))
    if diagonal is not None:
        slopes = jnp.where(diagonal, -slopes, slopes)
    return slopes.astype(jnp.bfloat16)


def across(a, b):
    return lax.dot_general(a, b, (((1,), (1,)), ((), ())), preferred_element_type=jnp.float32)


def gathered(buffer, pieces):
    row = 0
    for ref, part, rows in pieces:
        buffer[row : row + rows, :] = ref[part * rows : (part + 1) * rows, :]
        row += rows


def pairs_of(rows, *triples):
    return [(ref, part, rows) for near, far, part in triples for ref in (near, far)]


def accumulated(left, columns, total, scale, bias, matches=()):
    rows = left.shape[0]
    wide = 256
    for j in range(columns.shape[0] // wide):
        chunk = columns[j * wide : (j + 1) * wide, :]
        scores = across(left, chunk)
        diagonal = None
        starts = [row for row, number in matches if number == j]
        if starts:
            row = lax.broadcasted_iota(jnp.int32, scores.shape, 0)
            column = lax.broadcasted_iota(jnp.int32, scores.shape, 1)
            diagonal = jnp.logical_and(column == row - starts[0], column < wide // 2)
        term = jnp.dot(slopes_of(scores, scale, bias, diagonal), chunk, preferred_element_type=jnp.float32)
        total = term if total is None else total + term
    return total


def early_kernel(scale, bias, left, first, w1, w1_far, acc, columns):
    rows = first.shape[0] // 2
    gathered(columns, [(first, 0, 2 * rows)])
    gathered(columns.at[2 * rows :, :], pairs_of(rows, (w1, w1_far, 0), (w1, w1_far, 1), (w1, w1_far, 2)))
    acc[...] = accumulated(left[...], columns, None, scale[0], bias[0], [(i * rows, i) for i in range(3)])


def middle_kernel(scale, bias, left, y1, y1_far, acc, out, columns):
    rows = y1.shape[0] // 2
    gathered(columns, pairs_of(rows, (y1, y1_far, 0), (y1, y1_far, 1)))
    out[...] = accumulated(left[...], columns, acc[...], scale[0], bias[0])


def late_kernel(parts, scale, bias, left, acc, last, last_far, out0, out1, columns):
    rows = out0.shape[0]
    gathered(columns, pairs_of(rows, (last, last_far, 0), (last, last_far, 1)))
    for part, out in zip(parts, (out0, out1)):
        here = slice(part * rows, (part + 1) * rows)
        total = accumulated(
            left[here, :], columns, acc[here, :], scale[0], bias[0], [(0, 0)] if part == CHIPS - 1 else []
        )
        out[...] = (scale[0] * total).astype(out.dtype)


def body(images, captions, scale, bias):
    rows, width = images.shape
    blocks = lax.axis_size("blk")
    chip = lax.axis_index("zl")
    low = chip < 2
    inner = jnp.logical_or(chip == 1, chip == 2)

    def line(array, pairs):
        return lax.ppermute(array, "zl", pairs)

    def swapped(array):
        return lax.ppermute(array, "core", [(0, 1), (1, 0)])

    def neighbour(array, chips):
        pairs = []
        for p in range(blocks):
            for k in chips:
                q = p + 1 if k % 2 else p - 1
                pairs.append(((q % blocks) * CHIPS + k, p * CHIPS + k))
        return lax.ppermute(array, ("blk", "zl"), pairs)

    f32 = functools.partial(jax.ShapeDtypeStruct, dtype=jnp.float32)
    b16 = functools.partial(jax.ShapeDtypeStruct, dtype=jnp.bfloat16)
    unit = 4 * rows * rows * width

    to_inner = [(0, 1), (3, 2)]
    between = [(1, 2), (2, 1)]
    to_far = [(0, 2), (3, 1)]

    own = jnp.where(low, captions, images)
    other = jnp.where(low, images, captions)
    both = jnp.concatenate([own, other])

    y0 = neighbour(jnp.where(inner, own, other), range(CHIPS))
    xe = line(both, to_inner)
    xo = line(both, between)
    own_far = swapped(own)
    af = line(own, to_far)

    to_near, to_last, w1, left, first = in_vmem(
        functools.partial(pack_kernel, rows),
        [b16((n * rows, width)) for n in (2, 2, 3, 4, 2)],
        own, other, own_far, xe, xo, y0, af,
    )
    y1 = neighbour(to_near, (1, 2))
    last = line(to_last, to_far)
    w1_far = swapped(w1)
    (acc,) = in_vmem(
        early_kernel, [f32((4 * rows, width))], scale, bias, left, first, w1, w1_far,
        flops=32 * unit, scalars=2, scratch=[b16((8 * rows, width))],
    )
    y1, acc = lax.optimization_barrier((y1, acc))
    y1_far = swapped(y1)
    (acc,) = in_vmem(
        middle_kernel, [f32((4 * rows, width))], scale, bias, left, y1, y1_far, acc,
        flops=16 * unit, scalars=2, scratch=[b16((4 * rows, width))],
    )
    last_far = swapped(last)
    oe, of = in_vmem(
        functools.partial(late_kernel, (1, 3)), [b16((rows, width))] * 2, scale, bias, left, acc, last, last_far,
        flops=8 * unit, scalars=2, scratch=[b16((4 * rows, width))],
    )
    om, oo = in_vmem(
        functools.partial(late_kernel, (0, 2)), [b16((rows, width))] * 2, scale, bias, left, acc, last, last_far,
        flops=8 * unit, scalars=2, scratch=[b16((4 * rows, width))],
    )

    to_end = line(oe, [(1, 0), (2, 3)])
    to_far_end = line(of, [(1, 3), (2, 0)])
    to_other = line(oo, between)
    own_result = jnp.where(inner, om, to_end)
    other_result = jnp.where(inner, to_other, to_far_end)
    return (jnp.where(low, own_result, other_result), jnp.where(low, other_result, own_result))


def solution(mesh):
    fine = Mesh(mesh.devices.reshape(-1, CHIPS, CORES), ("blk", "zl", "core"))
    rows = P(("blk", "zl", "core"), None)
    return jax.shard_map(
        body, mesh=fine, in_specs=(rows, rows, P(), P()), out_specs=(rows, rows), check_vma=False
    )
```

```python
import functools
import math

import jax
import jax.numpy as jnp
from jax import lax
from jax.experimental import pallas as pl
from jax.experimental.pallas import tpu as pltpu
from jax.sharding import Mesh, PartitionSpec as P

CHIPS = 4
CORES = 2
GROUPS = 3
LIMIT = 12 * 1024 * 1024


def in_vmem(kernel, shapes, *operands, flops=0, scalars=0, scratch=()):
    moved_bytes = sum(math.prod(s.shape) * s.dtype.itemsize for s in shapes)
    return pl.pallas_call(
        kernel,
        out_shape=shapes,
        in_specs=[pl.BlockSpec(memory_space=pltpu.SMEM)] * scalars
        + [pl.BlockSpec(memory_space=pltpu.VMEM)] * (len(operands) - scalars),
        out_specs=[pl.BlockSpec(memory_space=pltpu.VMEM)] * len(shapes),
        scratch_shapes=[pltpu.VMEM(s.shape, s.dtype) for s in scratch],
        compiler_params=pltpu.CompilerParams(vmem_limit_bytes=LIMIT),
        cost_estimate=pl.CostEstimate(flops=flops, bytes_accessed=moved_bytes, transcendentals=0),
    )(*operands)


def pack_kernel(rows, own, other, xe, xo, y0, to_near, to_last, w1):
    gathered(to_near, [(xe, 0, rows), (xo, 1, rows)])
    gathered(to_last, [(other, 0, rows), (y0, 0, rows)])
    gathered(w1, [(own, 0, rows), (xe, 0, rows), (xo, 1, rows)])


def slopes_of(scores, scale, bias, diagonal=None):
    scores = scores * scale + bias
    if diagonal is not None:
        scores = jnp.where(diagonal, -scores, scores)
    slopes = 1.0 / (1.0 + jnp.exp(-scores))
    if diagonal is not None:
        slopes = jnp.where(diagonal, -slopes, slopes)
    return slopes.astype(jnp.bfloat16)


def across(a, b):
    return lax.dot_general(a, b, (((1,), (1,)), ((), ())), preferred_element_type=jnp.float32)


def at_inner():
    chip = lax.axis_index("zl")
    return jnp.logical_or(chip == 1, chip == 2)


def at_border(group):
    chip, place = lax.axis_index("zl"), lax.rem(lax.axis_index("blk"), group)
    return jnp.logical_or(
        jnp.logical_and(place == group - 1, chip == 2), jnp.logical_and(place == 0, chip == 1)
    )


def gathered(buffer, pieces):
    row = 0
    for ref, part, rows in pieces:
        buffer[row : row + rows, :] = ref[part * rows : (part + 1) * rows, :]
        row += rows


def pairs_of(rows, *triples):
    return [(ref, part, rows) for near, far, part in triples for ref in (near, far)]


def accumulated(left, columns, total, scale, bias, matches=()):
    rows = left.shape[0]
    wide = 256
    for j in range(columns.shape[0] // wide):
        chunk = columns[j * wide : (j + 1) * wide, :]
        scores = across(left, chunk)
        diagonal = None
        starts = [row for row, number in matches if number == j]
        if starts:
            row = lax.broadcasted_iota(jnp.int32, scores.shape, 0)
            column = lax.broadcasted_iota(jnp.int32, scores.shape, 1)
            diagonal = jnp.logical_and(column == row - starts[0], column < wide // 2)
        term = jnp.dot(slopes_of(scores, scale, bias, diagonal), chunk, preferred_element_type=jnp.float32)
        total = term if total is None else total + term
    return total


def early_kernel(scale, bias, am, xe, xo, af, w1, w1_far, left, acc, columns):
    @pl.when(at_inner())
    def _():
        rows = am.shape[0]
        gathered(left, [(am, 0, rows), (xe, 1, rows), (xo, 0, rows), (af, 0, rows)])
        gathered(columns, pairs_of(rows, *((w1, w1_far, i) for i in range(3))))
        acc[...] = accumulated(left[...], columns, None, scale[0], bias[0], [(i * rows, i) for i in range(3)])


def second_pack_kernel(group, y1, last, y0, ka, kb, w2):
    rows = y0.shape[0]
    gathered(w2, [(y1, 0, 2 * rows), (last, 0, 2 * rows), (y0, 0, rows)])

    @pl.when(at_border(group))
    def _():
        gathered(w2.at[3 * rows :, :], [(kb, 0, rows), (ka, 0, rows)])


def late_kernel(parts, scale, bias, left, acc, w2, w2_far, out0, out1, columns):
    @pl.when(at_inner())
    def _():
        rows = out0.shape[0]
        gathered(columns, pairs_of(rows, *((w2, w2_far, i) for i in range(5))))
        for part, out in zip(parts, (out0, out1)):
            here = slice(part * rows, (part + 1) * rows)
            matches = [(0, 2)] if part == CHIPS - 1 else []
            total = accumulated(left[here, :], columns, acc[here, :], scale[0], bias[0], matches)
            out[...] = (scale[0] * total).astype(out.dtype)


def body(images, captions, scale, bias):
    rows, width = images.shape
    blocks = lax.axis_size("blk")
    chip = lax.axis_index("zl")
    low = chip < 2
    inner = jnp.logical_or(chip == 1, chip == 2)

    def line(array, pairs):
        return lax.ppermute(array, "zl", pairs)

    group = blocks // GROUPS
    def swapped(array):
        pairs = [(chip * CORES + core, chip * CORES + 1 - core) for chip in (1, 2) for core in (0, 1)]
        return lax.ppermute(array, ("zl", "core"), pairs)

    def swapped_at_border(array):
        pairs = []
        for p in range(0, blocks, group):
            for place in (p * CHIPS + 1, (p + group - 1) * CHIPS + 2):
                pairs += [(place * CORES, place * CORES + 1), (place * CORES + 1, place * CORES)]
        return lax.ppermute(array, ("blk", "zl", "core"), pairs)

    def neighbour(array):
        pairs = []
        for p in range(blocks):
            pairs.append((((p + 1) % blocks) * CHIPS + 2, p * CHIPS + 2))
            pairs.append((((p - 1) % blocks) * CHIPS + 1, p * CHIPS + 1))
        return lax.ppermute(array, ("blk", "zl"), pairs)

    def neighbour_in_group(array):
        pairs = []
        for p in range(blocks):
            start = p - p % group
            for k in range(CHIPS):
                q = start + (p - start + (-1 if k % 2 else 1)) % group
                pairs.append((q * CHIPS + k, p * CHIPS + k))
        return lax.ppermute(array, ("blk", "zl"), pairs)

    def across_groups(array, low_source, high_source):
        pairs = []
        for p in range(0, blocks, group):
            q = p + group - 1
            pairs.append((((q + group) % blocks) * CHIPS + low_source, q * CHIPS + 2))
            pairs.append((((p - group) % blocks) * CHIPS + high_source, p * CHIPS + 1))
        return lax.ppermute(array, ("blk", "zl"), pairs)

    f32 = functools.partial(jax.ShapeDtypeStruct, dtype=jnp.float32)
    b16 = functools.partial(jax.ShapeDtypeStruct, dtype=jnp.bfloat16)
    unit = 4 * rows * rows * width

    to_inner = [(0, 1), (3, 2)]
    between = [(1, 2), (2, 1)]
    to_far = [(0, 2), (3, 1)]

    own = jnp.where(low, images, captions)
    other = jnp.where(low, captions, images)
    both = jnp.concatenate([own, other])
    xe = line(both, to_inner)
    xo = line(both, between)
    af = line(own, to_far)
    y0 = neighbour_in_group(jnp.where(inner, own, other))

    to_near, to_last, w1 = in_vmem(
        functools.partial(pack_kernel, rows), [b16((n * rows, width)) for n in (2, 2, 3)], own, other, xe, xo, y0
    )
    af, y0, w1, to_near, to_last = lax.optimization_barrier((af, y0, w1, to_near, to_last))
    y1 = neighbour(to_near)
    ka = across_groups(y0, 2, 1)
    kb = across_groups(y0, 0, 3)
    last = line(to_last, to_far)
    w1_far = swapped(w1)
    left, acc = in_vmem(
        early_kernel, [b16((4 * rows, width)), f32((4 * rows, width))],
        scale, bias, other, xe, xo, af, w1, w1_far,
        flops=24 * unit, scalars=2, scratch=[b16((6 * rows, width))],
    )
    y1, last, ka, kb, acc = lax.optimization_barrier((y1, last, ka, kb, acc))
    (w2,) = in_vmem(
        functools.partial(second_pack_kernel, group), [b16((5 * rows, width))], y1, last, y0, ka, kb
    )
    w2_far = swapped(w2)
    oe, of = in_vmem(
        functools.partial(late_kernel, (1, 3)), [b16((rows, width))] * 2, scale, bias, left, acc, w2, w2_far,
        flops=20 * unit, scalars=2, scratch=[b16((10 * rows, width))],
    )
    om, oo = in_vmem(
        functools.partial(late_kernel, (0, 2)), [b16((rows, width))] * 2, scale, bias, left, acc, w2, w2_far,
        flops=20 * unit, scalars=2, scratch=[b16((10 * rows, width))],
    )

    to_end = line(oe, [(1, 0), (2, 3)])
    to_far_end = line(of, [(1, 3), (2, 0)])
    to_other = line(oo, between)
    own_result = jnp.where(inner, om, to_end)
    other_result = jnp.where(inner, to_other, to_far_end)
    return (jnp.where(low, other_result, own_result), jnp.where(low, own_result, other_result))


def solution(mesh):
    fine = Mesh(mesh.devices.reshape(-1, CHIPS, CORES), ("blk", "zl", "core"))
    rows = P(("blk", "zl", "core"), None)
    return jax.shard_map(
        body, mesh=fine, in_specs=(rows, rows, P(), P()), out_specs=(rows, rows), check_vma=False
    )
```

```python
import functools
import math

import jax
import jax.numpy as jnp
from jax import lax
from jax.experimental import pallas as pl
from jax.experimental.pallas import tpu as pltpu
from jax.sharding import Mesh, PartitionSpec as P

CHIPS = 4
CORES = 2
GROUPS = 3
LIMIT = 12 * 1024 * 1024


def in_vmem(kernel, shapes, *operands, flops=0, scalars=0, scratch=()):
    moved_bytes = sum(math.prod(s.shape) * s.dtype.itemsize for s in shapes)
    return pl.pallas_call(
        kernel,
        out_shape=shapes,
        in_specs=[pl.BlockSpec(memory_space=pltpu.SMEM)] * scalars
        + [pl.BlockSpec(memory_space=pltpu.VMEM)] * (len(operands) - scalars),
        out_specs=[pl.BlockSpec(memory_space=pltpu.VMEM)] * len(shapes),
        scratch_shapes=[pltpu.VMEM(s.shape, s.dtype) for s in scratch],
        compiler_params=pltpu.CompilerParams(vmem_limit_bytes=LIMIT),
        cost_estimate=pl.CostEstimate(flops=flops, bytes_accessed=moved_bytes, transcendentals=0),
    )(*operands)


def pack_kernel(rows, other, xe, xo, y0, to_near, to_last):
    gathered(to_near, [(xe, 0, rows), (xo, 1, rows)])
    gathered(to_last, [(other, 0, rows), (y0, 0, rows)])


def slopes_of(scores, scale, bias, diagonal=None):
    scores = scores * scale + bias
    if diagonal is not None:
        scores = jnp.where(diagonal, -scores, scores)
    slopes = 1.0 / (1.0 + jnp.exp(-scores))
    if diagonal is not None:
        slopes = jnp.where(diagonal, -slopes, slopes)
    return slopes.astype(jnp.bfloat16)


def across(a, b):
    return lax.dot_general(a, b, (((1,), (1,)), ((), ())), preferred_element_type=jnp.float32)


def at_inner():
    chip = lax.axis_index("zl")
    return jnp.logical_or(chip == 1, chip == 2)


def at_border(group):
    chip, place = lax.axis_index("zl"), lax.rem(lax.axis_index("blk"), group)
    return jnp.logical_or(
        jnp.logical_and(place == group - 1, chip == 2), jnp.logical_and(place == 0, chip == 1)
    )


def at_late(group):
    chip, block, blocks = lax.axis_index("zl"), lax.axis_index("blk"), lax.axis_size("blk")
    upper = jnp.logical_and(lax.rem(block, group) == 0, block > 0)
    return jnp.logical_or(
        jnp.logical_and(block == blocks - 1, chip == 2), jnp.logical_and(upper, chip == 1)
    )


def gathered(buffer, pieces):
    row = 0
    for ref, part, rows in pieces:
        buffer[row : row + rows, :] = ref[part * rows : (part + 1) * rows, :]
        row += rows


def pairs_of(rows, *triples):
    return [(ref, part, rows) for near, far, part in triples for ref in (near, far)]


def accumulated(left, columns, total, scale, bias, matches=()):
    rows = left.shape[0]
    wide = 256
    for j in range(columns.shape[0] // wide):
        chunk = columns[j * wide : (j + 1) * wide, :]
        scores = across(left, chunk)
        diagonal = None
        starts = [row for row, number in matches if number == j]
        if starts:
            row = lax.broadcasted_iota(jnp.int32, scores.shape, 0)
            column = lax.broadcasted_iota(jnp.int32, scores.shape, 1)
            diagonal = jnp.logical_and(column == row - starts[0], column < wide // 2)
        term = jnp.dot(slopes_of(scores, scale, bias, diagonal), chunk, preferred_element_type=jnp.float32)
        total = term if total is None else total + term
    return total


def early_kernel(scale, bias, am, xe, xo, af, own, own_far, w1, w1_far, left, acc, columns):
    @pl.when(at_inner())
    def _():
        rows = am.shape[0]
        gathered(left, [(am, 0, rows), (xe, 1, rows), (xo, 0, rows), (af, 0, rows)])
        gathered(columns, pairs_of(rows, (own, own_far, 0), (w1, w1_far, 0), (w1, w1_far, 1)))
        acc[...] = accumulated(left[...], columns, None, scale[0], bias[0], [(i * rows, i) for i in range(3)])


def second_pack_kernel(group, y1, y2, last, y0, ka, kb, w2):
    rows = y0.shape[0]
    gathered(w2, [(y1, 0, 2 * rows), (last, 0, 2 * rows), (y0, 0, rows)])

    @pl.when(at_border(group))
    def _():
        gathered(w2.at[3 * rows :, :], [(kb, 0, rows), (ka, 0, rows)])

    @pl.when(at_late(group))
    def _():
        gathered(w2, [(y2, 0, 2 * rows)])


def late_kernel(parts, scale, bias, left, acc, w2, w2_far, out0, out1, columns):
    @pl.when(at_inner())
    def _():
        rows = out0.shape[0]
        gathered(columns, pairs_of(rows, *((w2, w2_far, i) for i in range(5))))
        for part, out in zip(parts, (out0, out1)):
            here = slice(part * rows, (part + 1) * rows)
            matches = [(0, 2)] if part == CHIPS - 1 else []
            total = accumulated(left[here, :], columns, acc[here, :], scale[0], bias[0], matches)
            out[...] = (scale[0] * total).astype(out.dtype)


def body(images, captions, scale, bias):
    rows, width = images.shape
    blocks = lax.axis_size("blk")
    chip = lax.axis_index("zl")
    low = chip < 2
    inner = jnp.logical_or(chip == 1, chip == 2)

    def line(array, pairs):
        return lax.ppermute(array, "zl", pairs)

    group = blocks // GROUPS
    def swapped(array):
        pairs = [(chip * CORES + core, chip * CORES + 1 - core) for chip in (1, 2) for core in (0, 1)]
        return lax.ppermute(array, ("zl", "core"), pairs)

    def swapped_at_border(array):
        pairs = []
        for p in range(0, blocks, group):
            for place in (p * CHIPS + 1, (p + group - 1) * CHIPS + 2):
                pairs += [(place * CORES, place * CORES + 1), (place * CORES + 1, place * CORES)]
        return lax.ppermute(array, ("blk", "zl", "core"), pairs)

    def neighbour(array, late):
        pairs = []
        for p in range(blocks):
            if (p == blocks - 1) == late:
                pairs.append((((p + 1) % blocks) * CHIPS + 2, p * CHIPS + 2))
            if (p % group == 0 and p > 0) == late:
                pairs.append((((p - 1) % blocks) * CHIPS + 1, p * CHIPS + 1))
        return lax.ppermute(array, ("blk", "zl"), pairs)

    def neighbour_in_group(array):
        pairs = []
        for p in range(blocks):
            start = p - p % group
            for k in range(CHIPS):
                q = start + (p - start + (-1 if k % 2 else 1)) % group
                pairs.append((q * CHIPS + k, p * CHIPS + k))
        return lax.ppermute(array, ("blk", "zl"), pairs)

    def across_groups(array, low_source, high_source):
        pairs = []
        for p in range(0, blocks, group):
            q = p + group - 1
            pairs.append((((q + group) % blocks) * CHIPS + low_source, q * CHIPS + 2))
            pairs.append((((p - group) % blocks) * CHIPS + high_source, p * CHIPS + 1))
        return lax.ppermute(array, ("blk", "zl"), pairs)

    f32 = functools.partial(jax.ShapeDtypeStruct, dtype=jnp.float32)
    b16 = functools.partial(jax.ShapeDtypeStruct, dtype=jnp.bfloat16)
    unit = 4 * rows * rows * width

    to_inner = [(0, 1), (3, 2)]
    between = [(1, 2), (2, 1)]
    to_far = [(0, 2), (3, 1)]

    own = jnp.where(low, images, captions)
    other = jnp.where(low, captions, images)
    both = jnp.concatenate([own, other])
    xe = line(both, to_inner)
    xo = line(both, between)
    af = line(own, to_far)
    y0 = neighbour_in_group(jnp.where(inner, own, other))

    own_far = swapped(own)
    to_near, to_last = in_vmem(
        functools.partial(pack_kernel, rows), [b16((2 * rows, width))] * 2, other, xe, xo, y0
    )
    af, own_far, y0, to_near, to_last = lax.optimization_barrier((af, own_far, y0, to_near, to_last))
    y1 = neighbour(to_near, False)
    last = line(to_last, to_far)
    kb = across_groups(y0, 0, 3)
    ka = across_groups(y0, 2, 1)
    y2 = neighbour(to_near, True)
    w1_far = swapped(to_near)
    left, acc = in_vmem(
        early_kernel, [b16((4 * rows, width)), f32((4 * rows, width))],
        scale, bias, other, xe, xo, af, own, own_far, to_near, w1_far,
        flops=24 * unit, scalars=2, scratch=[b16((6 * rows, width))],
    )
    y1, last, kb, ka, acc = lax.optimization_barrier((y1, last, kb, ka, acc))
    y1, last, kb, ka, y2 = lax.optimization_barrier((y1, last, kb, ka, y2))
    (w2,) = in_vmem(
        functools.partial(second_pack_kernel, group), [b16((5 * rows, width))], y1, y2, last, y0, ka, kb
    )
    w2_far = swapped(w2)
    oe, of = in_vmem(
        functools.partial(late_kernel, (1, 3)), [b16((rows, width))] * 2, scale, bias, left, acc, w2, w2_far,
        flops=20 * unit, scalars=2, scratch=[b16((10 * rows, width))],
    )
    om, oo = in_vmem(
        functools.partial(late_kernel, (0, 2)), [b16((rows, width))] * 2, scale, bias, left, acc, w2, w2_far,
        flops=20 * unit, scalars=2, scratch=[b16((10 * rows, width))],
    )

    to_end = line(oe, [(1, 0), (2, 3)])
    to_far_end = line(of, [(1, 3), (2, 0)])
    to_other = line(oo, between)
    own_result = jnp.where(inner, om, to_end)
    other_result = jnp.where(inner, to_other, to_far_end)
    return (jnp.where(low, other_result, own_result), jnp.where(low, own_result, other_result))


def solution(mesh):
    fine = Mesh(mesh.devices.reshape(-1, CHIPS, CORES), ("blk", "zl", "core"))
    rows = P(("blk", "zl", "core"), None)
    return jax.shard_map(
        body, mesh=fine, in_specs=(rows, rows, P(), P()), out_specs=(rows, rows), check_vma=False
    )
```

```python
import functools
import math

import jax
import jax.numpy as jnp
from jax import lax
from jax.experimental import pallas as pl
from jax.experimental.pallas import tpu as pltpu
from jax.sharding import Mesh, PartitionSpec as P

CHIPS = 4
CORES = 2
GROUPS = 3
LIMIT = 12 * 1024 * 1024


def in_vmem(kernel, shapes, *operands, flops=0, scalars=0, scratch=()):
    moved_bytes = sum(math.prod(s.shape) * s.dtype.itemsize for s in shapes)
    return pl.pallas_call(
        kernel,
        out_shape=shapes,
        in_specs=[pl.BlockSpec(memory_space=pltpu.SMEM)] * scalars
        + [pl.BlockSpec(memory_space=pltpu.VMEM)] * (len(operands) - scalars),
        out_specs=[pl.BlockSpec(memory_space=pltpu.VMEM)] * len(shapes),
        scratch_shapes=[pltpu.VMEM(s.shape, s.dtype) for s in scratch],
        compiler_params=pltpu.CompilerParams(vmem_limit_bytes=LIMIT),
        cost_estimate=pl.CostEstimate(flops=flops, bytes_accessed=moved_bytes, transcendentals=0),
    )(*operands)


def pack_kernel(rows, other, xe, xo, y0, to_near, to_last):
    gathered(to_near, [(xe, 0, rows), (xo, 1, rows)])
    gathered(to_last, [(other, 0, rows), (y0, 0, rows)])


def slopes_of(scores, scale, bias, diagonal=None):
    scores = scores * scale + bias
    if diagonal is not None:
        scores = jnp.where(diagonal, -scores, scores)
    slopes = 1.0 / (1.0 + jnp.exp(-scores))
    if diagonal is not None:
        slopes = jnp.where(diagonal, -slopes, slopes)
    return slopes.astype(jnp.bfloat16)


def across(a, b):
    return lax.dot_general(a, b, (((1,), (1,)), ((), ())), preferred_element_type=jnp.float32)


def at_inner():
    chip = lax.axis_index("zl")
    return jnp.logical_or(chip == 1, chip == 2)


def at_border(group):
    chip, place = lax.axis_index("zl"), lax.rem(lax.axis_index("blk"), group)
    return jnp.logical_or(
        jnp.logical_and(place == group - 1, chip == 2), jnp.logical_and(place == 0, chip == 1)
    )


def at_late(group):
    chip, block, blocks = lax.axis_index("zl"), lax.axis_index("blk"), lax.axis_size("blk")
    upper = jnp.logical_and(lax.rem(block, group) == 0, block > 0)
    return jnp.logical_or(
        jnp.logical_and(block == blocks - 1, chip == 2), jnp.logical_and(upper, chip == 1)
    )


def gathered(buffer, pieces):
    row = 0
    for ref, part, rows in pieces:
        buffer[row : row + rows, :] = ref[part * rows : (part + 1) * rows, :]
        row += rows


def pairs_of(rows, *triples):
    return [(ref, part, rows) for near, far, part in triples for ref in (near, far)]


def accumulated(left, columns, total, scale, bias, matches=()):
    rows = left.shape[0]
    wide = 256
    for j in range(columns.shape[0] // wide):
        chunk = columns[j * wide : (j + 1) * wide, :]
        scores = across(left, chunk)
        diagonal = None
        starts = [row for row, number in matches if number == j]
        if starts:
            row = lax.broadcasted_iota(jnp.int32, scores.shape, 0)
            column = lax.broadcasted_iota(jnp.int32, scores.shape, 1)
            diagonal = jnp.logical_and(column == row - starts[0], column < wide // 2)
        term = jnp.dot(slopes_of(scores, scale, bias, diagonal), chunk, preferred_element_type=jnp.float32)
        total = term if total is None else total + term
    return total


def early_kernel(scale, bias, am, xe, xo, af, own, own_far, w1, w1_far, left, acc, columns):
    @pl.when(at_inner())
    def _():
        rows = am.shape[0]
        gathered(left, [(am, 0, rows), (xe, 1, rows), (xo, 0, rows), (af, 0, rows)])
        gathered(columns, pairs_of(rows, (own, own_far, 0), (w1, w1_far, 0), (w1, w1_far, 1)))
        acc[...] = accumulated(left[...], columns, None, scale[0], bias[0], [(i * rows, i) for i in range(3)])


def second_pack_kernel(group, y1, y2, last, y0, ka, kb, w2):
    rows = y0.shape[0]
    gathered(w2, [(y1, 0, 2 * rows), (last, 0, 2 * rows), (y0, 0, rows)])

    @pl.when(at_border(group))
    def _():
        gathered(w2.at[3 * rows :, :], [(kb, 0, rows), (ka, 0, rows)])

    @pl.when(at_late(group))
    def _():
        gathered(w2, [(y2, 0, 2 * rows)])


def late_kernel(start, scale, bias, left, acc, w2, w2_far, *outs_and_columns):
    @pl.when(at_inner())
    def _():
        *outs, columns = outs_and_columns
        rows = outs[0].shape[0]
        gathered(columns, pairs_of(rows, *((w2, w2_far, i) for i in range(5))))
        here = slice(start * rows, (start + len(outs)) * rows)
        matches = [(0, 2)] if start == CHIPS - 1 else []
        total = scale[0] * accumulated(left[here, :], columns, acc[here, :], scale[0], bias[0], matches)
        for i, out in enumerate(outs):
            out[...] = total[i * rows : (i + 1) * rows, :].astype(out.dtype)


def body(images, captions, scale, bias):
    rows, width = images.shape
    blocks = lax.axis_size("blk")
    chip = lax.axis_index("zl")
    low = chip < 2
    inner = jnp.logical_or(chip == 1, chip == 2)

    def line(array, pairs):
        return lax.ppermute(array, "zl", pairs)

    group = blocks // GROUPS
    def swapped(array):
        pairs = [(chip * CORES + core, chip * CORES + 1 - core) for chip in (1, 2) for core in (0, 1)]
        return lax.ppermute(array, ("zl", "core"), pairs)

    def swapped_at_border(array):
        pairs = []
        for p in range(0, blocks, group):
            for place in (p * CHIPS + 1, (p + group - 1) * CHIPS + 2):
                pairs += [(place * CORES, place * CORES + 1), (place * CORES + 1, place * CORES)]
        return lax.ppermute(array, ("blk", "zl", "core"), pairs)

    def neighbour(array, late):
        pairs = []
        for p in range(blocks):
            if (p == blocks - 1) == late:
                pairs.append((((p + 1) % blocks) * CHIPS + 2, p * CHIPS + 2))
            if (p % group == 0 and p > 0) == late:
                pairs.append((((p - 1) % blocks) * CHIPS + 1, p * CHIPS + 1))
        return lax.ppermute(array, ("blk", "zl"), pairs)

    def neighbour_in_group(array):
        pairs = []
        for p in range(blocks):
            start = p - p % group
            for k in range(CHIPS):
                q = start + (p - start + (-1 if k % 2 else 1)) % group
                pairs.append((q * CHIPS + k, p * CHIPS + k))
        return lax.ppermute(array, ("blk", "zl"), pairs)

    def across_groups(array, low_source, high_source):
        pairs = []
        for p in range(0, blocks, group):
            q = p + group - 1
            pairs.append((((q + group) % blocks) * CHIPS + low_source, q * CHIPS + 2))
            pairs.append((((p - group) % blocks) * CHIPS + high_source, p * CHIPS + 1))
        return lax.ppermute(array, ("blk", "zl"), pairs)

    f32 = functools.partial(jax.ShapeDtypeStruct, dtype=jnp.float32)
    b16 = functools.partial(jax.ShapeDtypeStruct, dtype=jnp.bfloat16)
    unit = 4 * rows * rows * width

    to_inner = [(0, 1), (3, 2)]
    between = [(1, 2), (2, 1)]
    to_far = [(0, 2), (3, 1)]

    own = jnp.where(low, images, captions)
    other = jnp.where(low, captions, images)
    both = jnp.concatenate([own, other])
    xe = line(both, to_inner)
    xo = line(both, between)
    af = line(own, to_far)
    y0 = neighbour_in_group(jnp.where(inner, own, other))

    own_far = swapped(own)
    to_near, to_last = in_vmem(
        functools.partial(pack_kernel, rows), [b16((2 * rows, width))] * 2, other, xe, xo, y0
    )
    af, own_far, y0, to_near, to_last = lax.optimization_barrier((af, own_far, y0, to_near, to_last))
    y1 = neighbour(to_near, False)
    last = line(to_last, to_far)
    kb = across_groups(y0, 0, 3)
    ka = across_groups(y0, 2, 1)
    y2 = neighbour(to_near, True)
    w1_far = swapped(to_near)
    left, acc = in_vmem(
        early_kernel, [b16((4 * rows, width)), f32((4 * rows, width))],
        scale, bias, other, xe, xo, af, own, own_far, to_near, w1_far,
        flops=24 * unit, scalars=2, scratch=[b16((6 * rows, width))],
    )
    y1, last, kb, ka, acc = lax.optimization_barrier((y1, last, kb, ka, acc))
    y1, last, kb, ka, y2 = lax.optimization_barrier((y1, last, kb, ka, y2))
    (w2,) = in_vmem(
        functools.partial(second_pack_kernel, group), [b16((5 * rows, width))], y1, y2, last, y0, ka, kb
    )
    w2_far = swapped(w2)
    (of,) = in_vmem(
        functools.partial(late_kernel, 3), [b16((rows, width))] * 1, scale, bias, left, acc, w2, w2_far,
        flops=10 * unit, scalars=2, scratch=[b16((10 * rows, width))],
    )
    oe, oo = in_vmem(
        functools.partial(late_kernel, 1), [b16((rows, width))] * 2, scale, bias, left, acc, w2, w2_far,
        flops=20 * unit, scalars=2, scratch=[b16((10 * rows, width))],
    )
    (om,) = in_vmem(
        functools.partial(late_kernel, 0), [b16((rows, width))] * 1, scale, bias, left, acc, w2, w2_far,
        flops=10 * unit, scalars=2, scratch=[b16((10 * rows, width))],
    )

    to_far_end = line(of, [(1, 3), (2, 0)])
    to_end = line(oe, [(1, 0), (2, 3)])
    to_other = line(oo, between)
    own_result = jnp.where(inner, om, to_end)
    other_result = jnp.where(inner, to_other, to_far_end)
    return (jnp.where(low, other_result, own_result), jnp.where(low, own_result, other_result))


def solution(mesh):
    fine = Mesh(mesh.devices.reshape(-1, CHIPS, CORES), ("blk", "zl", "core"))
    rows = P(("blk", "zl", "core"), None)
    return jax.shard_map(
        body, mesh=fine, in_specs=(rows, rows, P(), P()), out_specs=(rows, rows), check_vma=False
    )
```

```python
import functools
import math

import jax
import jax.numpy as jnp
from jax import lax
from jax.experimental import pallas as pl
from jax.experimental.pallas import tpu as pltpu
from jax.sharding import Mesh, PartitionSpec as P

CHIPS = 4
CORES = 2
GROUPS = 3
LIMIT = 12 * 1024 * 1024


def in_vmem(kernel, shapes, *operands, flops=0, scalars=0, scratch=()):
    moved_bytes = sum(math.prod(s.shape) * s.dtype.itemsize for s in shapes)
    return pl.pallas_call(
        kernel,
        out_shape=shapes,
        in_specs=[pl.BlockSpec(memory_space=pltpu.SMEM)] * scalars
        + [pl.BlockSpec(memory_space=pltpu.VMEM)] * (len(operands) - scalars),
        out_specs=[pl.BlockSpec(memory_space=pltpu.VMEM)] * len(shapes),
        scratch_shapes=[pltpu.VMEM(s.shape, s.dtype) for s in scratch],
        compiler_params=pltpu.CompilerParams(vmem_limit_bytes=LIMIT),
        cost_estimate=pl.CostEstimate(flops=flops, bytes_accessed=moved_bytes, transcendentals=0),
    )(*operands)


def pack_kernel(group, other, xe, xo, af, y0, to_near, to_last, to_group):
    rows = other.shape[0]
    gathered(to_near, [(xe, 0, rows), (xo, 1, rows)])
    gathered(to_last, [(other, 0, rows), (y0, 0, rows)])
    to_group[...] = to_near[...]

    @pl.when(sends_down(group))
    def _():
        gathered(to_group, [(af, 0, rows), (other, 0, rows)])


def slopes_of(scores, scale, bias, diagonal=None):
    scores = scores * scale + bias
    if diagonal is not None:
        scores = jnp.where(diagonal, -scores, scores)
    slopes = 1.0 / (1.0 + jnp.exp(-scores))
    if diagonal is not None:
        slopes = jnp.where(diagonal, -slopes, slopes)
    return slopes.astype(jnp.bfloat16)


def across(a, b):
    return lax.dot_general(a, b, (((1,), (1,)), ((), ())), preferred_element_type=jnp.float32)


def at_inner():
    chip = lax.axis_index("zl")
    return jnp.logical_or(chip == 1, chip == 2)


def at_border(group):
    chip, place = lax.axis_index("zl"), lax.rem(lax.axis_index("blk"), group)
    return jnp.logical_or(
        jnp.logical_and(place == group - 1, chip == 2), jnp.logical_and(place == 0, chip == 1)
    )


def sends_down(group):
    chip, block, blocks = lax.axis_index("zl"), lax.axis_index("blk"), lax.axis_size("blk")
    lower = jnp.logical_and(lax.rem(block, group) == 0, block > 0)
    return jnp.logical_or(
        jnp.logical_and(block == blocks - 1, chip == 2), jnp.logical_and(lower, chip == 1)
    )


def gathered(buffer, pieces):
    row = 0
    for ref, part, rows in pieces:
        buffer[row : row + rows, :] = ref[part * rows : (part + 1) * rows, :]
        row += rows


def pairs_of(rows, *triples):
    return [(ref, part, rows) for near, far, part in triples for ref in (near, far)]


def accumulated(left, columns, total, scale, bias, matches=()):
    rows = left.shape[0]
    wide = 256
    for j in range(columns.shape[0] // wide):
        chunk = columns[j * wide : (j + 1) * wide, :]
        scores = across(left, chunk)
        diagonal = None
        starts = [row for row, number in matches if number == j]
        if starts:
            row = lax.broadcasted_iota(jnp.int32, scores.shape, 0)
            column = lax.broadcasted_iota(jnp.int32, scores.shape, 1)
            diagonal = jnp.logical_and(column == row - starts[0], column < wide // 2)
        term = jnp.dot(slopes_of(scores, scale, bias, diagonal), chunk, preferred_element_type=jnp.float32)
        total = term if total is None else total + term
    return total


def early_kernel(scale, bias, am, xe, xo, af, own, own_far, w1, w1_far, left, acc, columns):
    @pl.when(at_inner())
    def _():
        rows = am.shape[0]
        gathered(left, [(am, 0, rows), (xe, 1, rows), (xo, 0, rows), (af, 0, rows)])
        gathered(columns, pairs_of(rows, (own, own_far, 0), (w1, w1_far, 0), (w1, w1_far, 1)))
        acc[...] = accumulated(left[...], columns, None, scale[0], bias[0], [(i * rows, i) for i in range(3)])


def second_pack_kernel(group, y1, y2, last, y0, ka, kb, w2):
    rows = y0.shape[0]
    gathered(w2, [(y1, 0, 2 * rows), (last, 0, 2 * rows), (y0, 0, rows)])

    @pl.when(at_border(group))
    def _():
        gathered(w2, [(y2, 0, 2 * rows)])
        gathered(w2.at[3 * rows :, :], [(kb, 0, rows), (ka, 0, rows)])


def late_kernel(start, scale, bias, left, acc, w2, w2_far, *outs_and_columns):
    @pl.when(at_inner())
    def _():
        *outs, columns = outs_and_columns
        rows = outs[0].shape[0]
        gathered(columns, pairs_of(rows, *((w2, w2_far, i) for i in range(5))))
        here = slice(start * rows, (start + len(outs)) * rows)
        matches = [(0, 2)] if start == CHIPS - 1 else []
        total = scale[0] * accumulated(left[here, :], columns, acc[here, :], scale[0], bias[0], matches)
        for i, out in enumerate(outs):
            out[...] = total[i * rows : (i + 1) * rows, :].astype(out.dtype)


def body(images, captions, scale, bias):
    rows, width = images.shape
    blocks = lax.axis_size("blk")
    chip = lax.axis_index("zl")
    low = chip < 2
    inner = jnp.logical_or(chip == 1, chip == 2)

    def line(array, pairs):
        return lax.ppermute(array, "zl", pairs)

    group = blocks // GROUPS
    def swapped(array):
        pairs = [(chip * CORES + core, chip * CORES + 1 - core) for chip in (1, 2) for core in (0, 1)]
        return lax.ppermute(array, ("zl", "core"), pairs)

    def swapped_at_border(array):
        pairs = []
        for p in range(0, blocks, group):
            for place in (p * CHIPS + 1, (p + group - 1) * CHIPS + 2):
                pairs += [(place * CORES, place * CORES + 1), (place * CORES + 1, place * CORES)]
        return lax.ppermute(array, ("blk", "zl", "core"), pairs)

    def neighbour(array):
        pairs = []
        for p in range(blocks):
            if (p + 1) % group:
                pairs.append(((p + 1) * CHIPS + 2, p * CHIPS + 2))
            if p % group:
                pairs.append(((p - 1) * CHIPS + 1, p * CHIPS + 1))
        return lax.ppermute(array, ("blk", "zl"), pairs)

    def between_groups(array):
        pairs = []
        for p in range(group - 1, blocks, group):
            q = (p + 1) % blocks
            pairs.append((q * CHIPS + (1 if q else 2), p * CHIPS + 2))
            pairs.append((p * CHIPS + (1 if q else 2), q * CHIPS + 1))
        return lax.ppermute(array, ("blk", "zl"), pairs)

    def neighbour_in_group(array):
        pairs = []
        for p in range(blocks):
            start = p - p % group
            for k in range(CHIPS):
                q = start + (p - start + (-1 if k % 2 else 1)) % group
                pairs.append((q * CHIPS + k, p * CHIPS + k))
        return lax.ppermute(array, ("blk", "zl"), pairs)

    def across_groups(array, low_source, high_source):
        pairs = []
        for p in range(0, blocks, group):
            q = p + group - 1
            pairs.append((((q + group) % blocks) * CHIPS + low_source, q * CHIPS + 2))
            pairs.append((((p - group) % blocks) * CHIPS + high_source, p * CHIPS + 1))
        return lax.ppermute(array, ("blk", "zl"), pairs)

    f32 = functools.partial(jax.ShapeDtypeStruct, dtype=jnp.float32)
    b16 = functools.partial(jax.ShapeDtypeStruct, dtype=jnp.bfloat16)
    unit = 4 * rows * rows * width

    to_inner = [(0, 1), (3, 2)]
    between = [(1, 2), (2, 1)]
    to_far = [(0, 2), (3, 1)]

    own = jnp.where(low, images, captions)
    other = jnp.where(low, captions, images)
    both = jnp.concatenate([own, other])
    xe = line(both, to_inner)
    xo = line(both, between)
    af = line(own, to_far)
    y0 = neighbour_in_group(jnp.where(inner, own, other))

    own_far = swapped(own)
    to_near, to_last, to_group = in_vmem(
        functools.partial(pack_kernel, group), [b16((2 * rows, width))] * 3, other, xe, xo, af, y0
    )
    af, own_far, y0, to_near, to_last, to_group = lax.optimization_barrier(
        (af, own_far, y0, to_near, to_last, to_group)
    )
    y1 = neighbour(to_near)
    last = line(to_last, to_far)
    kb = across_groups(y0, 0, 3)
    ka = across_groups(y0, 2, 1)
    y2 = between_groups(to_group)
    w1_far = swapped(to_near)
    left, acc = in_vmem(
        early_kernel, [b16((4 * rows, width)), f32((4 * rows, width))],
        scale, bias, other, xe, xo, af, own, own_far, to_near, w1_far,
        flops=24 * unit, scalars=2, scratch=[b16((6 * rows, width))],
    )
    y1, last, kb, ka, acc = lax.optimization_barrier((y1, last, kb, ka, acc))
    y1, last, kb, ka, y2 = lax.optimization_barrier((y1, last, kb, ka, y2))
    (w2,) = in_vmem(
        functools.partial(second_pack_kernel, group), [b16((5 * rows, width))], y1, y2, last, y0, ka, kb
    )
    w2_far = swapped(w2)
    (of,) = in_vmem(
        functools.partial(late_kernel, 3), [b16((rows, width))] * 1, scale, bias, left, acc, w2, w2_far,
        flops=10 * unit, scalars=2, scratch=[b16((10 * rows, width))],
    )
    oe, oo = in_vmem(
        functools.partial(late_kernel, 1), [b16((rows, width))] * 2, scale, bias, left, acc, w2, w2_far,
        flops=20 * unit, scalars=2, scratch=[b16((10 * rows, width))],
    )
    (om,) = in_vmem(
        functools.partial(late_kernel, 0), [b16((rows, width))] * 1, scale, bias, left, acc, w2, w2_far,
        flops=10 * unit, scalars=2, scratch=[b16((10 * rows, width))],
    )

    to_far_end = line(of, [(1, 3), (2, 0)])
    to_end = line(oe, [(1, 0), (2, 3)])
    to_other = line(oo, between)
    to_end, to_far_end = lax.optimization_barrier((to_end, to_far_end))
    to_end, to_other = lax.optimization_barrier((to_end, to_other))
    own_result = jnp.where(inner, om, to_end)
    other_result = jnp.where(inner, to_other, to_far_end)
    return (jnp.where(low, other_result, own_result), jnp.where(low, own_result, other_result))


def solution(mesh):
    fine = Mesh(mesh.devices.reshape(-1, CHIPS, CORES), ("blk", "zl", "core"))
    rows = P(("blk", "zl", "core"), None)
    return jax.shard_map(
        body, mesh=fine, in_specs=(rows, rows, P(), P()), out_specs=(rows, rows), check_vma=False
    )
```

```python
import functools
import math

import jax
import jax.numpy as jnp
from jax import lax
from jax.experimental import pallas as pl
from jax.experimental.pallas import tpu as pltpu
from jax.sharding import Mesh, PartitionSpec as P

CHIPS = 4
CORES = 2
GROUPS = 3
LIMIT = 12 * 1024 * 1024


def in_vmem(kernel, shapes, *operands, flops=0, scalars=0, scratch=()):
    moved_bytes = sum(math.prod(s.shape) * s.dtype.itemsize for s in shapes)
    return pl.pallas_call(
        kernel,
        out_shape=shapes,
        in_specs=[pl.BlockSpec(memory_space=pltpu.SMEM)] * scalars
        + [pl.BlockSpec(memory_space=pltpu.VMEM)] * (len(operands) - scalars),
        out_specs=[pl.BlockSpec(memory_space=pltpu.VMEM)] * len(shapes),
        scratch_shapes=[pltpu.VMEM(s.shape, s.dtype) for s in scratch],
        compiler_params=pltpu.CompilerParams(vmem_limit_bytes=LIMIT),
        cost_estimate=pl.CostEstimate(flops=flops, bytes_accessed=moved_bytes, transcendentals=0),
    )(*operands)


def pack_kernel(group, other, xe, xo, af, y0, to_near, to_last, to_group):
    rows = other.shape[0]
    gathered(to_near, [(xe, 0, rows), (xo, 1, rows)])
    gathered(to_last, [(other, 0, rows), (y0, 0, rows)])
    to_group[...] = to_near[...]

    @pl.when(sends_down(group))
    def _():
        gathered(to_group, [(af, 0, rows), (other, 0, rows)])


def slopes_of(scores, scale, bias, diagonal=None):
    scores = scores * scale + bias
    if diagonal is not None:
        scores = jnp.where(diagonal, -scores, scores)
    slopes = 1.0 / (1.0 + jnp.exp(-scores))
    if diagonal is not None:
        slopes = jnp.where(diagonal, -slopes, slopes)
    return slopes.astype(jnp.bfloat16)


def across(a, b):
    return lax.dot_general(a, b, (((1,), (1,)), ((), ())), preferred_element_type=jnp.float32)


def at_inner():
    chip = lax.axis_index("zl")
    return jnp.logical_or(chip == 1, chip == 2)


def at_border(group):
    chip, place = lax.axis_index("zl"), lax.rem(lax.axis_index("blk"), group)
    return jnp.logical_or(
        jnp.logical_and(place == group - 1, chip == 2), jnp.logical_and(place == 0, chip == 1)
    )


def sends_down(group):
    chip, block, blocks = lax.axis_index("zl"), lax.axis_index("blk"), lax.axis_size("blk")
    lower = jnp.logical_and(lax.rem(block, group) == 0, block > 0)
    return jnp.logical_or(
        jnp.logical_and(block == blocks - 1, chip == 2), jnp.logical_and(lower, chip == 1)
    )


def gathered(buffer, pieces):
    row = 0
    for ref, part, rows in pieces:
        buffer[row : row + rows, :] = ref[part * rows : (part + 1) * rows, :]
        row += rows


def pairs_of(rows, *triples):
    return [(ref, part, rows) for near, far, part in triples for ref in (near, far)]


def accumulated(left, columns, total, scale, bias, matches=()):
    wide = 256
    for start in range(0, columns.shape[0], wide):
        chunk = columns[start : min(start + wide, columns.shape[0]), :]
        scores = across(left, chunk)
        diagonal = None
        for first_row, first_column in matches:
            if start <= first_column < start + wide:
                row = lax.broadcasted_iota(jnp.int32, scores.shape, 0) - first_row
                column = lax.broadcasted_iota(jnp.int32, scores.shape, 1) - (first_column - start)
                inside = jnp.logical_and(column >= 0, column < wide // 2)
                diagonal = jnp.logical_and(column == row, inside)
        term = jnp.dot(slopes_of(scores, scale, bias, diagonal), chunk, preferred_element_type=jnp.float32)
        total = term if total is None else total + term
    return total


def early_kernel(scale, bias, am, xe, xo, af, own, own_far, w1, w1_far, left, acc, columns):
    @pl.when(at_inner())
    def _():
        rows = am.shape[0]
        gathered(left, [(am, 0, rows), (xe, 1, rows), (xo, 0, rows), (af, 0, rows)])
        gathered(columns, pairs_of(rows, (own, own_far, 0), (w1, w1_far, 0), (w1, w1_far, 1)))
        acc[...] = accumulated(left[...], columns, None, scale[0], bias[0], [(i * rows, 2 * i * rows) for i in range(3)])


def second_pack_kernel(group, y1, y2, last, y0, ka, kb, w2):
    rows = y0.shape[0]
    gathered(w2, [(y1, 0, 2 * rows), (last, 0, 2 * rows), (y0, 0, rows)])

    @pl.when(at_border(group))
    def _():
        gathered(w2, [(y2, 0, 2 * rows)])
        gathered(w2.at[3 * rows :, :], [(kb, 0, rows), (ka, 0, rows)])


def near_kernel(scale, bias, left, acc, w2, out):
    @pl.when(at_inner())
    def _():
        rows = left.shape[0] // CHIPS
        out[...] = accumulated(left[...], w2, acc[...], scale[0], bias[0], [(3 * rows, 2 * rows)])


def late_kernel(start, scale, bias, left, acc, w2_far, *outs):
    @pl.when(at_inner())
    def _():
        rows = outs[0].shape[0]
        here = slice(start * rows, (start + len(outs)) * rows)
        total = scale[0] * accumulated(left[here, :], w2_far, acc[here, :], scale[0], bias[0])
        for i, out in enumerate(outs):
            out[...] = total[i * rows : (i + 1) * rows, :].astype(out.dtype)


def body(images, captions, scale, bias):
    rows, width = images.shape
    blocks = lax.axis_size("blk")
    chip = lax.axis_index("zl")
    low = chip < 2
    inner = jnp.logical_or(chip == 1, chip == 2)

    def line(array, pairs):
        return lax.ppermute(array, "zl", pairs)

    group = blocks // GROUPS
    def swapped(array):
        pairs = [(chip * CORES + core, chip * CORES + 1 - core) for chip in (1, 2) for core in (0, 1)]
        return lax.ppermute(array, ("zl", "core"), pairs)

    def swapped_at_border(array):
        pairs = []
        for p in range(0, blocks, group):
            for place in (p * CHIPS + 1, (p + group - 1) * CHIPS + 2):
                pairs += [(place * CORES, place * CORES + 1), (place * CORES + 1, place * CORES)]
        return lax.ppermute(array, ("blk", "zl", "core"), pairs)

    def neighbour(array):
        pairs = []
        for p in range(blocks):
            if (p + 1) % group:
                pairs.append(((p + 1) * CHIPS + 2, p * CHIPS + 2))
            if p % group:
                pairs.append(((p - 1) * CHIPS + 1, p * CHIPS + 1))
        return lax.ppermute(array, ("blk", "zl"), pairs)

    def between_groups(array):
        pairs = []
        for p in range(group - 1, blocks, group):
            q = (p + 1) % blocks
            pairs.append((q * CHIPS + (1 if q else 2), p * CHIPS + 2))
            pairs.append((p * CHIPS + (1 if q else 2), q * CHIPS + 1))
        return lax.ppermute(array, ("blk", "zl"), pairs)

    def neighbour_in_group(array):
        pairs = []
        for p in range(blocks):
            start = p - p % group
            for k in range(CHIPS):
                q = start + (p - start + (-1 if k % 2 else 1)) % group
                pairs.append((q * CHIPS + k, p * CHIPS + k))
        return lax.ppermute(array, ("blk", "zl"), pairs)

    def across_groups(array, low_source, high_source):
        pairs = []
        for p in range(0, blocks, group):
            q = p + group - 1
            pairs.append((((q + group) % blocks) * CHIPS + low_source, q * CHIPS + 2))
            pairs.append((((p - group) % blocks) * CHIPS + high_source, p * CHIPS + 1))
        return lax.ppermute(array, ("blk", "zl"), pairs)

    f32 = functools.partial(jax.ShapeDtypeStruct, dtype=jnp.float32)
    b16 = functools.partial(jax.ShapeDtypeStruct, dtype=jnp.bfloat16)
    unit = 4 * rows * rows * width

    to_inner = [(0, 1), (3, 2)]
    between = [(1, 2), (2, 1)]
    to_far = [(0, 2), (3, 1)]

    own = jnp.where(low, images, captions)
    other = jnp.where(low, captions, images)
    both = jnp.concatenate([own, other])
    xe = line(both, to_inner)
    xo = line(both, between)
    af = line(own, to_far)
    y0 = neighbour_in_group(jnp.where(inner, own, other))

    own_far = swapped(own)
    to_near, to_last, to_group = in_vmem(
        functools.partial(pack_kernel, group), [b16((2 * rows, width))] * 3, other, xe, xo, af, y0
    )
    af, own_far, y0, to_near, to_last, to_group = lax.optimization_barrier(
        (af, own_far, y0, to_near, to_last, to_group)
    )
    y1 = neighbour(to_near)
    last = line(to_last, to_far)
    kb = across_groups(y0, 0, 3)
    ka = across_groups(y0, 2, 1)
    y2 = between_groups(to_group)
    w1_far = swapped(to_near)
    left, acc = in_vmem(
        early_kernel, [b16((4 * rows, width)), f32((4 * rows, width))],
        scale, bias, other, xe, xo, af, own, own_far, to_near, w1_far,
        flops=24 * unit, scalars=2, scratch=[b16((6 * rows, width))],
    )
    y1, last, kb, ka, acc = lax.optimization_barrier((y1, last, kb, ka, acc))
    y1, last, kb, ka, y2 = lax.optimization_barrier((y1, last, kb, ka, y2))
    (w2,) = in_vmem(
        functools.partial(second_pack_kernel, group), [b16((5 * rows, width))], y1, y2, last, y0, ka, kb
    )
    w2_far = swapped(w2)
    (acc,) = in_vmem(
        near_kernel, [f32((4 * rows, width))], scale, bias, left, acc, w2, flops=20 * unit, scalars=2
    )
    (of,) = in_vmem(
        functools.partial(late_kernel, 3), [b16((rows, width))] * 1, scale, bias, left, acc, w2_far,
        flops=5 * unit, scalars=2,
    )
    oe, oo = in_vmem(
        functools.partial(late_kernel, 1), [b16((rows, width))] * 2, scale, bias, left, acc, w2_far,
        flops=10 * unit, scalars=2,
    )
    (om,) = in_vmem(
        functools.partial(late_kernel, 0), [b16((rows, width))] * 1, scale, bias, left, acc, w2_far,
        flops=5 * unit, scalars=2,
    )

    to_far_end = line(of, [(1, 3), (2, 0)])
    to_end = line(oe, [(1, 0), (2, 3)])
    to_other = line(oo, between)
    to_end, to_far_end = lax.optimization_barrier((to_end, to_far_end))
    to_end, to_other = lax.optimization_barrier((to_end, to_other))
    own_result = jnp.where(inner, om, to_end)
    other_result = jnp.where(inner, to_other, to_far_end)
    return (jnp.where(low, other_result, own_result), jnp.where(low, own_result, other_result))


def solution(mesh):
    fine = Mesh(mesh.devices.reshape(-1, CHIPS, CORES), ("blk", "zl", "core"))
    rows = P(("blk", "zl", "core"), None)
    return jax.shard_map(
        body, mesh=fine, in_specs=(rows, rows, P(), P()), out_specs=(rows, rows), check_vma=False
    )
```

```python
import functools
import math

import jax
import jax.numpy as jnp
from jax import lax
from jax.experimental import pallas as pl
from jax.experimental.pallas import tpu as pltpu
from jax.sharding import Mesh, PartitionSpec as P

CHIPS = 4
CORES = 2
GROUPS = 3
LIMIT = 12 * 1024 * 1024


def in_vmem(kernel, shapes, *operands, flops=0, scalars=0, scratch=()):
    moved_bytes = sum(math.prod(s.shape) * s.dtype.itemsize for s in shapes)
    return pl.pallas_call(
        kernel,
        out_shape=shapes,
        in_specs=[pl.BlockSpec(memory_space=pltpu.SMEM)] * scalars
        + [pl.BlockSpec(memory_space=pltpu.VMEM)] * (len(operands) - scalars),
        out_specs=[pl.BlockSpec(memory_space=pltpu.VMEM)] * len(shapes),
        scratch_shapes=[pltpu.VMEM(s.shape, s.dtype) for s in scratch],
        compiler_params=pltpu.CompilerParams(vmem_limit_bytes=LIMIT),
        cost_estimate=pl.CostEstimate(flops=flops, bytes_accessed=moved_bytes, transcendentals=0),
    )(*operands)


def pack_kernel(group, other, xe, xo, af, y0, to_near, to_last, to_group):
    rows = other.shape[0]
    gathered(to_near, [(xe, 0, rows), (xo, 1, rows)])
    gathered(to_last, [(other, 0, rows), (y0, 0, rows)])
    to_group[...] = to_near[...]

    @pl.when(sends_down(group))
    def _():
        gathered(to_group, [(af, 0, rows), (other, 0, rows)])


def slopes_of(scores, scale, bias, diagonal=None):
    scores = scores * scale + bias
    if diagonal is not None:
        scores = jnp.where(diagonal, -scores, scores)
    slopes = 1.0 / (1.0 + jnp.exp(-scores))
    if diagonal is not None:
        slopes = jnp.where(diagonal, -slopes, slopes)
    return slopes.astype(jnp.bfloat16)


def across(a, b):
    return lax.dot_general(a, b, (((1,), (1,)), ((), ())), preferred_element_type=jnp.float32)


def at_inner():
    chip = lax.axis_index("zl")
    return jnp.logical_or(chip == 1, chip == 2)


def at_border(group):
    chip, place = lax.axis_index("zl"), lax.rem(lax.axis_index("blk"), group)
    return jnp.logical_or(
        jnp.logical_and(place == group - 1, chip == 2), jnp.logical_and(place == 0, chip == 1)
    )


def sends_down(group):
    chip, block, blocks = lax.axis_index("zl"), lax.axis_index("blk"), lax.axis_size("blk")
    lower = jnp.logical_and(lax.rem(block, group) == 0, block > 0)
    return jnp.logical_or(
        jnp.logical_and(block == blocks - 1, chip == 2), jnp.logical_and(lower, chip == 1)
    )


def gathered(buffer, pieces):
    row = 0
    for ref, part, rows in pieces:
        buffer[row : row + rows, :] = ref[part * rows : (part + 1) * rows, :]
        row += rows


def pairs_of(rows, *triples):
    return [(ref, part, rows) for near, far, part in triples for ref in (near, far)]


def accumulated(left, columns, total, scale, bias, matches=()):
    wide = 256
    for start in range(0, columns.shape[0], wide):
        chunk = columns[start : min(start + wide, columns.shape[0]), :]
        scores = across(left, chunk)
        diagonal = None
        for first_row, first_column in matches:
            if start <= first_column < start + wide:
                row = lax.broadcasted_iota(jnp.int32, scores.shape, 0) - first_row
                column = lax.broadcasted_iota(jnp.int32, scores.shape, 1) - (first_column - start)
                inside = jnp.logical_and(column >= 0, column < wide // 2)
                diagonal = jnp.logical_and(column == row, inside)
        term = jnp.dot(slopes_of(scores, scale, bias, diagonal), chunk, preferred_element_type=jnp.float32)
        total = term if total is None else total + term
    return total


def early_kernel(scale, bias, am, xe, xo, af, own, own_far, w1, w1_far, left, acc, columns):
    @pl.when(at_inner())
    def _():
        rows = am.shape[0]
        gathered(left, [(am, 0, rows), (xe, 1, rows), (xo, 0, rows), (af, 0, rows)])
        gathered(columns, pairs_of(rows, (own, own_far, 0), (w1, w1_far, 0), (w1, w1_far, 1)))
        acc[...] = accumulated(left[...], columns, None, scale[0], bias[0], [(i * rows, 2 * i * rows) for i in range(3)])


def second_pack_kernel(group, y1, y2, last, y0, ka, kb, w2):
    rows = y0.shape[0]
    gathered(w2, [(y1, 0, 2 * rows), (last, 0, 2 * rows), (y0, 0, rows)])

    @pl.when(at_border(group))
    def _():
        gathered(w2, [(y2, 0, 2 * rows)])
        gathered(w2.at[3 * rows :, :], [(kb, 0, rows), (ka, 0, rows)])


def near_kernel(scale, bias, left, acc, w2, out):
    @pl.when(at_inner())
    def _():
        rows = left.shape[0] // CHIPS
        out[...] = accumulated(left[...], w2, acc[...], scale[0], bias[0], [(3 * rows, 2 * rows)])


def late_kernel(start, scale, bias, left, acc, w2_far, *outs):
    @pl.when(at_inner())
    def _():
        rows = outs[0].shape[0]
        here = slice(start * rows, (start + len(outs)) * rows)
        total = scale[0] * accumulated(left[here, :], w2_far, acc[here, :], scale[0], bias[0])
        for i, out in enumerate(outs):
            out[...] = total[i * rows : (i + 1) * rows, :].astype(out.dtype)


def body(images, captions, scale, bias):
    rows, width = images.shape
    blocks = lax.axis_size("blk")
    chip = lax.axis_index("zl")
    low = chip < 2
    inner = jnp.logical_or(chip == 1, chip == 2)

    def line(array, pairs):
        return lax.ppermute(array, "zl", pairs)

    group = blocks // GROUPS
    def swapped(array):
        pairs = [(chip * CORES + core, chip * CORES + 1 - core) for chip in (1, 2) for core in (0, 1)]
        return lax.ppermute(array, ("zl", "core"), pairs)

    def swapped_at_border(array):
        pairs = []
        for p in range(0, blocks, group):
            for place in (p * CHIPS + 1, (p + group - 1) * CHIPS + 2):
                pairs += [(place * CORES, place * CORES + 1), (place * CORES + 1, place * CORES)]
        return lax.ppermute(array, ("blk", "zl", "core"), pairs)

    def neighbour(array):
        pairs = []
        for p in range(blocks):
            if (p + 1) % group:
                pairs.append(((p + 1) * CHIPS + 2, p * CHIPS + 2))
            if p % group:
                pairs.append(((p - 1) * CHIPS + 1, p * CHIPS + 1))
        return lax.ppermute(array, ("blk", "zl"), pairs)

    def between_groups(array):
        pairs = []
        for p in range(group - 1, blocks, group):
            q = (p + 1) % blocks
            pairs.append((q * CHIPS + (1 if q else 2), p * CHIPS + 2))
            pairs.append((p * CHIPS + (1 if q else 2), q * CHIPS + 1))
        return lax.ppermute(array, ("blk", "zl"), pairs)

    def neighbour_in_group(array):
        pairs = []
        for p in range(blocks):
            start = p - p % group
            for k in range(CHIPS):
                q = start + (p - start + (-1 if k % 2 else 1)) % group
                pairs.append((q * CHIPS + k, p * CHIPS + k))
        return lax.ppermute(array, ("blk", "zl"), pairs)

    def across_groups(array, low_source, high_source):
        pairs = []
        for p in range(0, blocks, group):
            q = p + group - 1
            pairs.append((((q + group) % blocks) * CHIPS + low_source, q * CHIPS + 2))
            pairs.append((((p - group) % blocks) * CHIPS + high_source, p * CHIPS + 1))
        return lax.ppermute(array, ("blk", "zl"), pairs)

    f32 = functools.partial(jax.ShapeDtypeStruct, dtype=jnp.float32)
    b16 = functools.partial(jax.ShapeDtypeStruct, dtype=jnp.bfloat16)
    unit = 4 * rows * rows * width

    to_inner = [(0, 1), (3, 2)]
    between = [(1, 2), (2, 1)]
    to_far = [(0, 2), (3, 1)]

    own = jnp.where(low, images, captions)
    other = jnp.where(low, captions, images)
    both = jnp.concatenate([own, other])
    xe = line(both, to_inner)
    xo = line(both, between)
    af = line(own, to_far)
    y0 = neighbour_in_group(jnp.where(inner, own, other))

    own_far = swapped(own)
    to_near, to_last, to_group = in_vmem(
        functools.partial(pack_kernel, group), [b16((2 * rows, width))] * 3, other, xe, xo, af, y0
    )
    af, own_far, y0, to_near, to_last, to_group = lax.optimization_barrier(
        (af, own_far, y0, to_near, to_last, to_group)
    )
    last = line(to_last, to_far)
    kb = across_groups(y0, 0, 3)
    ka = across_groups(y0, 2, 1)
    y2 = between_groups(to_group)
    w1_far = swapped(to_near)
    w1_far, inside = lax.optimization_barrier((w1_far, to_near))
    y1 = neighbour(inside)
    left, acc = in_vmem(
        early_kernel, [b16((4 * rows, width)), f32((4 * rows, width))],
        scale, bias, other, xe, xo, af, own, own_far, to_near, w1_far,
        flops=24 * unit, scalars=2, scratch=[b16((6 * rows, width))],
    )
    last, y2, kb, ka, y1, acc = lax.optimization_barrier((last, y2, kb, ka, y1, acc))
    (w2,) = in_vmem(
        functools.partial(second_pack_kernel, group), [b16((5 * rows, width))], y1, y2, last, y0, ka, kb
    )
    w2_far = swapped(w2)
    (acc,) = in_vmem(
        near_kernel, [f32((4 * rows, width))], scale, bias, left, acc, w2, flops=20 * unit, scalars=2
    )
    (oe,) = in_vmem(
        functools.partial(late_kernel, 1), [b16((rows, width))] * 1, scale, bias, left, acc, w2_far,
        flops=5 * unit, scalars=2,
    )
    (of,) = in_vmem(
        functools.partial(late_kernel, 3), [b16((rows, width))] * 1, scale, bias, left, acc, w2_far,
        flops=5 * unit, scalars=2,
    )
    (oo,) = in_vmem(
        functools.partial(late_kernel, 2), [b16((rows, width))] * 1, scale, bias, left, acc, w2_far,
        flops=5 * unit, scalars=2,
    )
    (om,) = in_vmem(
        functools.partial(late_kernel, 0), [b16((rows, width))] * 1, scale, bias, left, acc, w2_far,
        flops=5 * unit, scalars=2,
    )

    to_far_end = line(of, [(1, 3), (2, 0)])
    to_end = line(oe, [(1, 0), (2, 3)])
    to_other = line(oo, between)
    own_result = jnp.where(inner, om, to_end)
    other_result = jnp.where(inner, to_other, to_far_end)
    return (jnp.where(low, other_result, own_result), jnp.where(low, own_result, other_result))


def solution(mesh):
    fine = Mesh(mesh.devices.reshape(-1, CHIPS, CORES), ("blk", "zl", "core"))
    rows = P(("blk", "zl", "core"), None)
    return jax.shard_map(
        body, mesh=fine, in_specs=(rows, rows, P(), P()), out_specs=(rows, rows), check_vma=False
    )
```

```python
import functools
import math

import jax
import jax.numpy as jnp
from jax import lax
from jax.experimental import pallas as pl
from jax.experimental.pallas import tpu as pltpu
from jax.sharding import Mesh, PartitionSpec as P

CHIPS = 4
CORES = 2
GROUPS = 3
LIMIT = 12 * 1024 * 1024


def in_vmem(kernel, shapes, *operands, flops=0, scalars=0, scratch=()):
    moved_bytes = sum(math.prod(s.shape) * s.dtype.itemsize for s in shapes)
    return pl.pallas_call(
        kernel,
        out_shape=shapes,
        in_specs=[pl.BlockSpec(memory_space=pltpu.SMEM)] * scalars
        + [pl.BlockSpec(memory_space=pltpu.VMEM)] * (len(operands) - scalars),
        out_specs=[pl.BlockSpec(memory_space=pltpu.VMEM)] * len(shapes),
        scratch_shapes=[pltpu.VMEM(s.shape, s.dtype) for s in scratch],
        compiler_params=pltpu.CompilerParams(vmem_limit_bytes=LIMIT),
        cost_estimate=pl.CostEstimate(flops=flops, bytes_accessed=moved_bytes, transcendentals=0),
    )(*operands)


def pack_kernel(group, other, xe, xo, af, y0, to_near, to_last, to_group):
    rows = other.shape[0]
    gathered(to_near, [(xe, 0, rows), (xo, 1, rows)])
    gathered(to_last, [(other, 0, rows), (y0, 0, rows)])
    to_group[...] = to_near[...]

    @pl.when(sends_down(group))
    def _():
        gathered(to_group, [(af, 0, rows), (other, 0, rows)])


def slopes_of(scores, scale, bias, diagonal=None):
    scores = scores * scale + bias
    if diagonal is not None:
        scores = jnp.where(diagonal, -scores, scores)
    slopes = 1.0 / (1.0 + jnp.exp(-scores))
    if diagonal is not None:
        slopes = jnp.where(diagonal, -slopes, slopes)
    return slopes.astype(jnp.bfloat16)


def across(a, b):
    return lax.dot_general(a, b, (((1,), (1,)), ((), ())), preferred_element_type=jnp.float32)


def at_inner():
    chip = lax.axis_index("zl")
    return jnp.logical_or(chip == 1, chip == 2)


def at_border(group):
    chip, place = lax.axis_index("zl"), lax.rem(lax.axis_index("blk"), group)
    return jnp.logical_or(
        jnp.logical_and(place == group - 1, chip == 2), jnp.logical_and(place == 0, chip == 1)
    )


def sends_down(group):
    chip, block, blocks = lax.axis_index("zl"), lax.axis_index("blk"), lax.axis_size("blk")
    lower = jnp.logical_and(lax.rem(block, group) == 0, block > 0)
    return jnp.logical_or(
        jnp.logical_and(block == blocks - 1, chip == 2), jnp.logical_and(lower, chip == 1)
    )


def gathered(buffer, pieces):
    row = 0
    for ref, part, rows in pieces:
        buffer[row : row + rows, :] = ref[part * rows : (part + 1) * rows, :]
        row += rows


def pairs_of(rows, *triples):
    return [(ref, part, rows) for near, far, part in triples for ref in (near, far)]


def accumulated(left, columns, total, scale, bias, matches=()):
    wide = 256
    for start in range(0, columns.shape[0], wide):
        chunk = columns[start : min(start + wide, columns.shape[0]), :]
        scores = across(left, chunk)
        diagonal = None
        for first_row, first_column in matches:
            if start <= first_column < start + wide:
                row = lax.broadcasted_iota(jnp.int32, scores.shape, 0) - first_row
                column = lax.broadcasted_iota(jnp.int32, scores.shape, 1) - (first_column - start)
                inside = jnp.logical_and(column >= 0, column < wide // 2)
                diagonal = jnp.logical_and(column == row, inside)
        term = jnp.dot(slopes_of(scores, scale, bias, diagonal), chunk, preferred_element_type=jnp.float32)
        total = term if total is None else total + term
    return total


def early_kernel(scale, bias, am, xe, xo, af, own, own_far, w1, w1_far, left, acc, columns):
    @pl.when(at_inner())
    def _():
        rows = am.shape[0]
        gathered(left, [(am, 0, rows), (xe, 1, rows), (xo, 0, rows), (af, 0, rows)])
        gathered(columns, pairs_of(rows, (own, own_far, 0), (w1, w1_far, 0), (w1, w1_far, 1)))
        acc[...] = accumulated(left[...], columns, None, scale[0], bias[0], [(i * rows, 2 * i * rows) for i in range(3)])


def sends_up(group):
    chip, block, blocks = lax.axis_index("zl"), lax.axis_index("blk"), lax.axis_size("blk")
    upper = jnp.logical_and(lax.rem(block, group) == group - 1, block < blocks - 1)
    return jnp.logical_or(jnp.logical_and(block == 0, chip == 2), jnp.logical_and(upper, chip == 1))


def second_pack_kernel(group, y1, y2, last, y0, ka, kb, w2):
    rows = y0.shape[0]
    gathered(w2, [(y1, 0, 2 * rows), (last, 0, 2 * rows), (y0, 0, rows)])

    @pl.when(jnp.logical_or(at_border(group), sends_up(group)))
    def _():
        gathered(w2, [(y2, 0, 2 * rows)])

    @pl.when(at_border(group))
    def _():
        gathered(w2.at[3 * rows :, :], [(kb, 0, rows), (ka, 0, rows)])


def near_kernel(scale, bias, left, acc, w2, out):
    @pl.when(at_inner())
    def _():
        rows = left.shape[0] // CHIPS
        out[...] = accumulated(left[...], w2, acc[...], scale[0], bias[0], [(3 * rows, 2 * rows)])


def late_kernel(start, scale, bias, left, acc, w2_far, *outs):
    @pl.when(at_inner())
    def _():
        rows = outs[0].shape[0]
        here = slice(start * rows, (start + len(outs)) * rows)
        total = scale[0] * accumulated(left[here, :], w2_far, acc[here, :], scale[0], bias[0])
        for i, out in enumerate(outs):
            out[...] = total[i * rows : (i + 1) * rows, :].astype(out.dtype)


def body(images, captions, scale, bias):
    rows, width = images.shape
    blocks = lax.axis_size("blk")
    chip = lax.axis_index("zl")
    low = chip < 2
    inner = jnp.logical_or(chip == 1, chip == 2)

    def line(array, pairs):
        return lax.ppermute(array, "zl", pairs)

    group = blocks // GROUPS
    def swapped(array):
        pairs = [(chip * CORES + core, chip * CORES + 1 - core) for chip in (1, 2) for core in (0, 1)]
        return lax.ppermute(array, ("zl", "core"), pairs)

    def swapped_at_border(array):
        pairs = []
        for p in range(0, blocks, group):
            for place in (p * CHIPS + 1, (p + group - 1) * CHIPS + 2):
                pairs += [(place * CORES, place * CORES + 1), (place * CORES + 1, place * CORES)]
        return lax.ppermute(array, ("blk", "zl", "core"), pairs)

    def neighbour(array):
        pairs = []
        for p in range(blocks):
            if (p + 1) % group and p > 0:
                pairs.append(((p + 1) * CHIPS + 2, p * CHIPS + 2))
            if p % group and ((p + 1) % group or p == blocks - 1):
                pairs.append(((p - 1) * CHIPS + 1, p * CHIPS + 1))
        return lax.ppermute(array, ("blk", "zl"), pairs)

    def between_groups(array):
        pairs = []
        for p in range(group - 1, blocks, group):
            q = (p + 1) % blocks
            pairs.append((q * CHIPS + (1 if q else 2), p * CHIPS + 2))
            pairs.append((p * CHIPS + (1 if q else 2), q * CHIPS + 1))
            pairs.append(((p - 1) * CHIPS + 1, p * CHIPS + 1) if q else (CHIPS + 2, 2))
        return lax.ppermute(array, ("blk", "zl"), pairs)

    def neighbour_in_group(array):
        pairs = []
        for p in range(blocks):
            start = p - p % group
            for k in range(CHIPS):
                q = start + (p - start + (-1 if k % 2 else 1)) % group
                pairs.append((q * CHIPS + k, p * CHIPS + k))
        return lax.ppermute(array, ("blk", "zl"), pairs)

    def across_groups(array, low_source, high_source):
        pairs = []
        for p in range(0, blocks, group):
            q = p + group - 1
            pairs.append((((q + group) % blocks) * CHIPS + low_source, q * CHIPS + 2))
            pairs.append((((p - group) % blocks) * CHIPS + high_source, p * CHIPS + 1))
        return lax.ppermute(array, ("blk", "zl"), pairs)

    f32 = functools.partial(jax.ShapeDtypeStruct, dtype=jnp.float32)
    b16 = functools.partial(jax.ShapeDtypeStruct, dtype=jnp.bfloat16)
    unit = 4 * rows * rows * width

    to_inner = [(0, 1), (3, 2)]
    between = [(1, 2), (2, 1)]
    to_far = [(0, 2), (3, 1)]

    own = jnp.where(low, images, captions)
    other = jnp.where(low, captions, images)
    both = jnp.concatenate([own, other])
    xe = line(both, to_inner)
    xo = line(both, between)
    af = line(own, to_far)
    y0 = neighbour_in_group(jnp.where(inner, own, other))

    own_far = swapped(own)
    to_near, to_last, to_group = in_vmem(
        functools.partial(pack_kernel, group), [b16((2 * rows, width))] * 3, other, xe, xo, af, y0
    )
    af, own_far, y0, to_near, to_last, to_group = lax.optimization_barrier(
        (af, own_far, y0, to_near, to_last, to_group)
    )
    last = line(to_last, to_far)
    kb = across_groups(y0, 0, 3)
    ka = across_groups(y0, 2, 1)
    y2 = between_groups(to_group)
    w1_far = swapped(to_near)
    w1_far, inside = lax.optimization_barrier((w1_far, to_near))
    y1 = neighbour(inside)
    left, acc = in_vmem(
        early_kernel, [b16((4 * rows, width)), f32((4 * rows, width))],
        scale, bias, other, xe, xo, af, own, own_far, to_near, w1_far,
        flops=24 * unit, scalars=2, scratch=[b16((6 * rows, width))],
    )
    last, y2, kb, ka, y1, acc = lax.optimization_barrier((last, y2, kb, ka, y1, acc))
    (w2,) = in_vmem(
        functools.partial(second_pack_kernel, group), [b16((5 * rows, width))], y1, y2, last, y0, ka, kb
    )
    w2_far = swapped(w2)
    (acc,) = in_vmem(
        near_kernel, [f32((4 * rows, width))], scale, bias, left, acc, w2, flops=20 * unit, scalars=2
    )
    (oe,) = in_vmem(
        functools.partial(late_kernel, 1), [b16((rows, width))] * 1, scale, bias, left, acc, w2_far,
        flops=5 * unit, scalars=2,
    )
    (of,) = in_vmem(
        functools.partial(late_kernel, 3), [b16((rows, width))] * 1, scale, bias, left, acc, w2_far,
        flops=5 * unit, scalars=2,
    )
    (oo,) = in_vmem(
        functools.partial(late_kernel, 2), [b16((rows, width))] * 1, scale, bias, left, acc, w2_far,
        flops=5 * unit, scalars=2,
    )
    (om,) = in_vmem(
        functools.partial(late_kernel, 0), [b16((rows, width))] * 1, scale, bias, left, acc, w2_far,
        flops=5 * unit, scalars=2,
    )

    to_far_end = line(of, [(1, 3), (2, 0)])
    to_end = line(oe, [(1, 0), (2, 3)])
    to_other = line(oo, between)
    own_result = jnp.where(inner, om, to_end)
    other_result = jnp.where(inner, to_other, to_far_end)
    return (jnp.where(low, other_result, own_result), jnp.where(low, own_result, other_result))


def solution(mesh):
    fine = Mesh(mesh.devices.reshape(-1, CHIPS, CORES), ("blk", "zl", "core"))
    rows = P(("blk", "zl", "core"), None)
    return jax.shard_map(
        body, mesh=fine, in_specs=(rows, rows, P(), P()), out_specs=(rows, rows), check_vma=False
    )
```

```python
import functools
import math

import jax
import jax.numpy as jnp
from jax import lax
from jax.experimental import pallas as pl
from jax.experimental.pallas import tpu as pltpu
from jax.sharding import Mesh, PartitionSpec as P

CHIPS = 4
CORES = 2
GROUPS = 3
LIMIT = 12 * 1024 * 1024


def in_vmem(kernel, shapes, *operands, flops=0, scalars=0, scratch=()):
    moved_bytes = sum(math.prod(s.shape) * s.dtype.itemsize for s in shapes)
    return pl.pallas_call(
        kernel,
        out_shape=shapes,
        in_specs=[pl.BlockSpec(memory_space=pltpu.SMEM)] * scalars
        + [pl.BlockSpec(memory_space=pltpu.VMEM)] * (len(operands) - scalars),
        out_specs=[pl.BlockSpec(memory_space=pltpu.VMEM)] * len(shapes),
        scratch_shapes=[pltpu.VMEM(s.shape, s.dtype) for s in scratch],
        compiler_params=pltpu.CompilerParams(vmem_limit_bytes=LIMIT),
        cost_estimate=pl.CostEstimate(flops=flops, bytes_accessed=moved_bytes, transcendentals=0),
    )(*operands)


def pack_kernel(group, other, xe, xo, af, y0, to_near, to_last, to_group):
    rows = other.shape[0]
    gathered(to_near, [(xe, 0, rows), (xo, 1, rows)])
    gathered(to_last, [(other, 0, rows), (y0, 0, rows)])
    to_group[...] = to_near[...]

    @pl.when(sends_down(group))
    def _():
        gathered(to_group, [(af, 0, rows), (other, 0, rows)])


def slopes_of(scores, scale, bias, diagonal=None):
    scores = scores * scale + bias
    if diagonal is not None:
        scores = jnp.where(diagonal, -scores, scores)
    slopes = 1.0 / (1.0 + jnp.exp(-scores))
    if diagonal is not None:
        slopes = jnp.where(diagonal, -slopes, slopes)
    return slopes.astype(jnp.bfloat16)


def across(a, b):
    return lax.dot_general(a, b, (((1,), (1,)), ((), ())), preferred_element_type=jnp.float32)


def at_inner():
    chip = lax.axis_index("zl")
    return jnp.logical_or(chip == 1, chip == 2)


def at_border(group):
    chip, place = lax.axis_index("zl"), lax.rem(lax.axis_index("blk"), group)
    return jnp.logical_or(
        jnp.logical_and(place == group - 1, chip == 2), jnp.logical_and(place == 0, chip == 1)
    )


def sends_down(group):
    chip, block, blocks = lax.axis_index("zl"), lax.axis_index("blk"), lax.axis_size("blk")
    lower = jnp.logical_and(lax.rem(block, group) == 0, block > 0)
    return jnp.logical_or(
        jnp.logical_and(block == blocks - 1, chip == 2), jnp.logical_and(lower, chip == 1)
    )


def gathered(buffer, pieces):
    row = 0
    for ref, part, rows in pieces:
        buffer[row : row + rows, :] = ref[part * rows : (part + 1) * rows, :]
        row += rows


def pairs_of(rows, *triples):
    return [(ref, part, rows) for near, far, part in triples for ref in (near, far)]


def accumulated(left, columns, total, scale, bias, matches=()):
    wide = 256
    for start in range(0, columns.shape[0], wide):
        chunk = columns[start : min(start + wide, columns.shape[0]), :]
        scores = across(left, chunk)
        diagonal = None
        for first_row, first_column in matches:
            if start <= first_column < start + wide:
                row = lax.broadcasted_iota(jnp.int32, scores.shape, 0) - first_row
                column = lax.broadcasted_iota(jnp.int32, scores.shape, 1) - (first_column - start)
                inside = jnp.logical_and(column >= 0, column < wide // 2)
                diagonal = jnp.logical_and(column == row, inside)
        term = jnp.dot(slopes_of(scores, scale, bias, diagonal), chunk, preferred_element_type=jnp.float32)
        total = term if total is None else total + term
    return total


def early_kernel(scale, bias, am, xe, xo, af, own, own_far, w1, w1_far, left, acc, columns):
    @pl.when(at_inner())
    def _():
        rows = am.shape[0]
        gathered(left, [(am, 0, rows), (xe, 1, rows), (xo, 0, rows), (af, 0, rows)])
        gathered(columns, pairs_of(rows, (own, own_far, 0), (w1, w1_far, 0), (w1, w1_far, 1)))
        acc[...] = accumulated(left[...], columns, None, scale[0], bias[0], [(i * rows, 2 * i * rows) for i in range(3)])


def sends_up(group):
    chip, block, blocks = lax.axis_index("zl"), lax.axis_index("blk"), lax.axis_size("blk")
    upper = jnp.logical_and(lax.rem(block, group) == group - 1, block < blocks - 1)
    return jnp.logical_or(jnp.logical_and(block == 0, chip == 2), jnp.logical_and(upper, chip == 1))


def second_pack_kernel(group, y1, y2, last, y0, ka, kb, w2):
    rows = y0.shape[0]
    gathered(w2, [(y1, 0, 2 * rows), (last, 0, 2 * rows), (y0, 0, rows)])

    @pl.when(jnp.logical_or(at_border(group), sends_up(group)))
    def _():
        gathered(w2, [(y2, 0, 2 * rows)])

    @pl.when(at_border(group))
    def _():
        gathered(w2.at[3 * rows :, :], [(kb, 0, rows), (ka, 0, rows)])


def near_kernel(scale, bias, left, acc, w2, out):
    @pl.when(at_inner())
    def _():
        rows = left.shape[0] // CHIPS
        out[...] = accumulated(left[...], w2, acc[...], scale[0], bias[0], [(3 * rows, 2 * rows)])


def late_kernel(start, scale, bias, left, acc, w2_far, *outs):
    @pl.when(at_inner())
    def _():
        rows = outs[0].shape[0]
        here = slice(start * rows, (start + len(outs)) * rows)
        total = scale[0] * accumulated(left[here, :], w2_far, acc[here, :], scale[0], bias[0])
        for i, out in enumerate(outs):
            out[...] = total[i * rows : (i + 1) * rows, :].astype(out.dtype)


def body(images, captions, scale, bias):
    rows, width = images.shape
    blocks = lax.axis_size("blk")
    chip = lax.axis_index("zl")
    low = chip < 2
    inner = jnp.logical_or(chip == 1, chip == 2)

    def line(array, pairs):
        return lax.ppermute(array, "zl", pairs)

    group = blocks // GROUPS
    def swapped(array):
        pairs = [(chip * CORES + core, chip * CORES + 1 - core) for chip in (1, 2) for core in (0, 1)]
        return lax.ppermute(array, ("zl", "core"), pairs)

    def swapped_at_border(array):
        pairs = []
        for p in range(0, blocks, group):
            for place in (p * CHIPS + 1, (p + group - 1) * CHIPS + 2):
                pairs += [(place * CORES, place * CORES + 1), (place * CORES + 1, place * CORES)]
        return lax.ppermute(array, ("blk", "zl", "core"), pairs)

    def neighbour(array):
        pairs = []
        for p in range(blocks):
            if (p + 1) % group and p > 0:
                pairs.append(((p + 1) * CHIPS + 2, p * CHIPS + 2))
            if p % group and ((p + 1) % group or p == blocks - 1):
                pairs.append(((p - 1) * CHIPS + 1, p * CHIPS + 1))
        return lax.ppermute(array, ("blk", "zl"), pairs)

    def between_groups(array):
        pairs = []
        for p in range(group - 1, blocks, group):
            q = (p + 1) % blocks
            pairs.append((q * CHIPS + (1 if q else 2), p * CHIPS + 2))
            pairs.append((p * CHIPS + (1 if q else 2), q * CHIPS + 1))
            pairs.append(((p - 1) * CHIPS + 1, p * CHIPS + 1) if q else (CHIPS + 2, 2))
        return lax.ppermute(array, ("blk", "zl"), pairs)

    def neighbour_in_group(array):
        pairs = []
        for p in range(blocks):
            start = p - p % group
            for k in range(CHIPS):
                q = start + (p - start + (-1 if k % 2 else 1)) % group
                pairs.append((q * CHIPS + k, p * CHIPS + k))
        return lax.ppermute(array, ("blk", "zl"), pairs)

    def across_groups(array, low_source, high_source):
        pairs = []
        for p in range(0, blocks, group):
            q = p + group - 1
            pairs.append((((q + group) % blocks) * CHIPS + low_source, q * CHIPS + 2))
            pairs.append((((p - group) % blocks) * CHIPS + high_source, p * CHIPS + 1))
        return lax.ppermute(array, ("blk", "zl"), pairs)

    f32 = functools.partial(jax.ShapeDtypeStruct, dtype=jnp.float32)
    b16 = functools.partial(jax.ShapeDtypeStruct, dtype=jnp.bfloat16)
    unit = 4 * rows * rows * width

    to_inner = [(0, 1), (3, 2)]
    between = [(1, 2), (2, 1)]
    to_far = [(0, 2), (3, 1)]

    own = jnp.where(low, images, captions)
    other = jnp.where(low, captions, images)
    both = jnp.concatenate([own, other])
    xe = line(both, to_inner)
    xo = line(both, between)
    af = line(own, to_far)
    y0 = neighbour_in_group(jnp.where(inner, own, other))

    own_far = swapped(own)
    to_near, to_last, to_group = in_vmem(
        functools.partial(pack_kernel, group), [b16((2 * rows, width))] * 3, other, xe, xo, af, y0
    )
    af, own_far, y0, to_near, to_last, to_group = lax.optimization_barrier(
        (af, own_far, y0, to_near, to_last, to_group)
    )
    last = line(to_last, to_far)
    y2 = between_groups(to_group)
    w1_far = swapped(to_near)
    w1_far, inside, y0_late = lax.optimization_barrier((w1_far, to_near, y0))
    y1 = neighbour(inside)
    kb = across_groups(y0_late, 0, 3)
    ka = across_groups(y0_late, 2, 1)
    left, acc = in_vmem(
        early_kernel, [b16((4 * rows, width)), f32((4 * rows, width))],
        scale, bias, other, xe, xo, af, own, own_far, to_near, w1_far,
        flops=400 * unit, scalars=2, scratch=[b16((6 * rows, width))],
    )
    last, y2, kb, ka, y1, acc = lax.optimization_barrier((last, y2, kb, ka, y1, acc))
    (w2,) = in_vmem(
        functools.partial(second_pack_kernel, group), [b16((5 * rows, width))], y1, y2, last, y0, ka, kb
    )
    w2_far = swapped(w2)
    (acc,) = in_vmem(
        near_kernel, [f32((4 * rows, width))], scale, bias, left, acc, w2, flops=20 * unit, scalars=2
    )
    (oe,) = in_vmem(
        functools.partial(late_kernel, 1), [b16((rows, width))] * 1, scale, bias, left, acc, w2_far,
        flops=5 * unit, scalars=2,
    )
    (of,) = in_vmem(
        functools.partial(late_kernel, 3), [b16((rows, width))] * 1, scale, bias, left, acc, w2_far,
        flops=5 * unit, scalars=2,
    )
    (oo,) = in_vmem(
        functools.partial(late_kernel, 2), [b16((rows, width))] * 1, scale, bias, left, acc, w2_far,
        flops=5 * unit, scalars=2,
    )
    (om,) = in_vmem(
        functools.partial(late_kernel, 0), [b16((rows, width))] * 1, scale, bias, left, acc, w2_far,
        flops=5 * unit, scalars=2,
    )

    to_far_end = line(of, [(1, 3), (2, 0)])
    to_end = line(oe, [(1, 0), (2, 3)])
    to_other = line(oo, between)
    own_result = jnp.where(inner, om, to_end)
    other_result = jnp.where(inner, to_other, to_far_end)
    return (jnp.where(low, other_result, own_result), jnp.where(low, own_result, other_result))


def solution(mesh):
    fine = Mesh(mesh.devices.reshape(-1, CHIPS, CORES), ("blk", "zl", "core"))
    rows = P(("blk", "zl", "core"), None)
    return jax.shard_map(
        body, mesh=fine, in_specs=(rows, rows, P(), P()), out_specs=(rows, rows), check_vma=False
    )
```

```python
import functools
import math

import jax
import jax.numpy as jnp
from jax import lax
from jax.experimental import pallas as pl
from jax.experimental.pallas import tpu as pltpu
from jax.sharding import Mesh, PartitionSpec as P

CHIPS = 4
CORES = 2
GROUPS = 3
LIMIT = 12 * 1024 * 1024


def in_vmem(kernel, shapes, *operands, flops=0, scalars=0, scratch=()):
    moved_bytes = sum(math.prod(s.shape) * s.dtype.itemsize for s in shapes)
    return pl.pallas_call(
        kernel,
        out_shape=shapes,
        in_specs=[pl.BlockSpec(memory_space=pltpu.SMEM)] * scalars
        + [pl.BlockSpec(memory_space=pltpu.VMEM)] * (len(operands) - scalars),
        out_specs=[pl.BlockSpec(memory_space=pltpu.VMEM)] * len(shapes),
        scratch_shapes=[pltpu.VMEM(s.shape, s.dtype) for s in scratch],
        compiler_params=pltpu.CompilerParams(vmem_limit_bytes=LIMIT),
        cost_estimate=pl.CostEstimate(flops=flops, bytes_accessed=moved_bytes, transcendentals=0),
    )(*operands)


def pack_kernel(group, other, xe, xo, af, y0, to_near, to_last, to_group):
    rows = other.shape[0]
    gathered(to_near, [(xe, 0, rows), (xo, 1, rows)])
    gathered(to_last, [(other, 0, rows), (y0, 0, rows)])
    to_group[...] = to_near[...]

    @pl.when(sends_down(group))
    def _():
        gathered(to_group, [(af, 0, rows), (other, 0, rows)])


def slopes_of(scores, scale, bias, diagonal=None):
    scores = scores * scale + bias
    if diagonal is not None:
        scores = jnp.where(diagonal, -scores, scores)
    slopes = 1.0 / (1.0 + jnp.exp(-scores))
    if diagonal is not None:
        slopes = jnp.where(diagonal, -slopes, slopes)
    return slopes.astype(jnp.bfloat16)


def across(a, b):
    return lax.dot_general(a, b, (((1,), (1,)), ((), ())), preferred_element_type=jnp.float32)


def at_inner():
    chip = lax.axis_index("zl")
    return jnp.logical_or(chip == 1, chip == 2)


def at_border(group):
    chip, place = lax.axis_index("zl"), lax.rem(lax.axis_index("blk"), group)
    return jnp.logical_or(
        jnp.logical_and(place == group - 1, chip == 2), jnp.logical_and(place == 0, chip == 1)
    )


def sends_down(group):
    chip, block, blocks = lax.axis_index("zl"), lax.axis_index("blk"), lax.axis_size("blk")
    lower = jnp.logical_and(lax.rem(block, group) == 0, block > 0)
    return jnp.logical_or(
        jnp.logical_and(block == blocks - 1, chip == 2), jnp.logical_and(lower, chip == 1)
    )


def gathered(buffer, pieces):
    row = 0
    for ref, part, rows in pieces:
        buffer[row : row + rows, :] = ref[part * rows : (part + 1) * rows, :]
        row += rows


def pairs_of(rows, *triples):
    return [(ref, part, rows) for near, far, part in triples for ref in (near, far)]


def accumulated(left, columns, total, scale, bias, matches=()):
    wide = 256
    for start in range(0, columns.shape[0], wide):
        chunk = columns[start : min(start + wide, columns.shape[0]), :]
        scores = across(left, chunk)
        diagonal = None
        for first_row, first_column in matches:
            if start <= first_column < start + wide:
                row = lax.broadcasted_iota(jnp.int32, scores.shape, 0) - first_row
                column = lax.broadcasted_iota(jnp.int32, scores.shape, 1) - (first_column - start)
                inside = jnp.logical_and(column >= 0, column < wide // 2)
                diagonal = jnp.logical_and(column == row, inside)
        term = jnp.dot(slopes_of(scores, scale, bias, diagonal), chunk, preferred_element_type=jnp.float32)
        total = term if total is None else total + term
    return total


def early_kernel(scale, bias, am, xe, xo, af, own, own_far, w1, w1_far, left, acc, columns):
    @pl.when(at_inner())
    def _():
        rows = am.shape[0]
        gathered(left, [(am, 0, rows), (xe, 1, rows), (xo, 0, rows), (af, 0, rows)])
        gathered(columns, pairs_of(rows, (own, own_far, 0), (w1, w1_far, 0), (w1, w1_far, 1)))
        acc[...] = accumulated(left[...], columns, None, scale[0], bias[0], [(i * rows, 2 * i * rows) for i in range(3)])


def sends_up(group):
    chip, block, blocks = lax.axis_index("zl"), lax.axis_index("blk"), lax.axis_size("blk")
    upper = jnp.logical_and(lax.rem(block, group) == group - 1, block < blocks - 1)
    return jnp.logical_or(jnp.logical_and(block == 0, chip == 2), jnp.logical_and(upper, chip == 1))


def second_pack_kernel(group, y1, y2, last, y0, ka, kb, w2):
    rows = y0.shape[0]
    gathered(w2, [(y1, 0, 2 * rows), (last, 0, 2 * rows), (y0, 0, rows)])

    @pl.when(jnp.logical_or(at_border(group), sends_up(group)))
    def _():
        gathered(w2, [(y2, 0, 2 * rows)])

    @pl.when(at_border(group))
    def _():
        gathered(w2.at[3 * rows :, :], [(kb, 0, rows), (ka, 0, rows)])


def near_kernel(scale, bias, left, acc, w2, out):
    @pl.when(at_inner())
    def _():
        rows = left.shape[0] // CHIPS
        out[...] = accumulated(left[...], w2, acc[...], scale[0], bias[0], [(3 * rows, 2 * rows)])


def late_kernel(start, scale, bias, left, acc, w2_far, *outs):
    @pl.when(at_inner())
    def _():
        rows = outs[0].shape[0]
        here = slice(start * rows, (start + len(outs)) * rows)
        total = scale[0] * accumulated(left[here, :], w2_far, acc[here, :], scale[0], bias[0])
        for i, out in enumerate(outs):
            out[...] = total[i * rows : (i + 1) * rows, :].astype(out.dtype)


def body(images, captions, scale, bias):
    rows, width = images.shape
    blocks = lax.axis_size("blk")
    chip = lax.axis_index("zl")
    low = chip < 2
    inner = jnp.logical_or(chip == 1, chip == 2)

    def line(array, pairs):
        return lax.ppermute(array, "zl", pairs)

    group = blocks // GROUPS
    def swapped(array):
        pairs = [(chip * CORES + core, chip * CORES + 1 - core) for chip in (1, 2) for core in (0, 1)]
        return lax.ppermute(array, ("zl", "core"), pairs)

    def swapped_at_border(array):
        pairs = []
        for p in range(0, blocks, group):
            for place in (p * CHIPS + 1, (p + group - 1) * CHIPS + 2):
                pairs += [(place * CORES, place * CORES + 1), (place * CORES + 1, place * CORES)]
        return lax.ppermute(array, ("blk", "zl", "core"), pairs)

    def neighbour(array):
        pairs = []
        for p in range(blocks):
            if (p + 1) % group and p > 0:
                pairs.append(((p + 1) * CHIPS + 2, p * CHIPS + 2))
            if p % group and ((p + 1) % group or p == blocks - 1):
                pairs.append(((p - 1) * CHIPS + 1, p * CHIPS + 1))
        return lax.ppermute(array, ("blk", "zl"), pairs)

    def between_groups(array):
        pairs = []
        for p in range(group - 1, blocks, group):
            q = (p + 1) % blocks
            pairs.append((q * CHIPS + (1 if q else 2), p * CHIPS + 2))
            pairs.append((p * CHIPS + (1 if q else 2), q * CHIPS + 1))
            pairs.append(((p - 1) * CHIPS + 1, p * CHIPS + 1) if q else (CHIPS + 2, 2))
        return lax.ppermute(array, ("blk", "zl"), pairs)

    def neighbour_in_group(array):
        pairs = []
        for p in range(blocks):
            start = p - p % group
            for k in range(CHIPS):
                q = start + (p - start + (-1 if k % 2 else 1)) % group
                pairs.append((q * CHIPS + k, p * CHIPS + k))
        return lax.ppermute(array, ("blk", "zl"), pairs)

    def across_groups(array, low_source, high_source):
        pairs = []
        for p in range(0, blocks, group):
            q = p + group - 1
            pairs.append((((q + group) % blocks) * CHIPS + low_source, q * CHIPS + 2))
            pairs.append((((p - group) % blocks) * CHIPS + high_source, p * CHIPS + 1))
        return lax.ppermute(array, ("blk", "zl"), pairs)

    f32 = functools.partial(jax.ShapeDtypeStruct, dtype=jnp.float32)
    b16 = functools.partial(jax.ShapeDtypeStruct, dtype=jnp.bfloat16)
    unit = 4 * rows * rows * width

    to_inner = [(0, 1), (3, 2)]
    between = [(1, 2), (2, 1)]
    to_far = [(0, 2), (3, 1)]

    own = jnp.where(low, images, captions)
    other = jnp.where(low, captions, images)
    both = jnp.concatenate([own, other])
    xe = line(both, to_inner)
    xo = line(both, between)
    af = line(own, to_far)
    y0 = neighbour_in_group(jnp.where(inner, own, other))

    own_far = swapped(own)
    to_near, to_last, to_group = in_vmem(
        functools.partial(pack_kernel, group), [b16((2 * rows, width))] * 3, other, xe, xo, af, y0
    )
    af, own_far, y0, to_near, to_last, to_group = lax.optimization_barrier(
        (af, own_far, y0, to_near, to_last, to_group)
    )
    last = line(to_last, to_far)
    kb = across_groups(y0, 0, 3)
    ka = across_groups(y0, 2, 1)
    y2 = between_groups(to_group)
    w1_far = swapped(to_near)
    w1_far, inside = lax.optimization_barrier((w1_far, to_near))
    y1 = neighbour(inside)
    left, acc = in_vmem(
        early_kernel, [b16((4 * rows, width)), f32((4 * rows, width))],
        scale, bias, other, xe, xo, af, own, own_far, to_near, w1_far,
        flops=24 * unit, scalars=2, scratch=[b16((6 * rows, width))],
    )
    last, y2, kb, ka, y1, acc = lax.optimization_barrier((last, y2, kb, ka, y1, acc))
    (w2,) = in_vmem(
        functools.partial(second_pack_kernel, group), [b16((5 * rows, width))], y1, y2, last, y0, ka, kb
    )
    w2_far = swapped(w2)
    (acc,) = in_vmem(
        near_kernel, [f32((4 * rows, width))], scale, bias, left, acc, w2, flops=20 * unit, scalars=2
    )
    (oe,) = in_vmem(
        functools.partial(late_kernel, 1), [b16((rows, width))] * 1, scale, bias, left, acc, w2_far,
        flops=5 * unit, scalars=2,
    )
    (of,) = in_vmem(
        functools.partial(late_kernel, 3), [b16((rows, width))] * 1, scale, bias, left, acc, w2_far,
        flops=5 * unit, scalars=2,
    )
    (oo,) = in_vmem(
        functools.partial(late_kernel, 2), [b16((rows, width))] * 1, scale, bias, left, acc, w2_far,
        flops=5 * unit, scalars=2,
    )
    (om,) = in_vmem(
        functools.partial(late_kernel, 0), [b16((rows, width))] * 1, scale, bias, left, acc, w2_far,
        flops=5 * unit, scalars=2,
    )

    to_far_end = line(of, [(1, 3), (2, 0)])
    to_end = line(oe, [(1, 0), (2, 3)])
    to_other = line(oo, between)
    to_end, to_far_end = lax.optimization_barrier((to_end, to_far_end))
    to_far_end, to_other = lax.optimization_barrier((to_far_end, to_other))
    own_result = jnp.where(inner, om, to_end)
    other_result = jnp.where(inner, to_other, to_far_end)
    return (jnp.where(low, other_result, own_result), jnp.where(low, own_result, other_result))


def solution(mesh):
    fine = Mesh(mesh.devices.reshape(-1, CHIPS, CORES), ("blk", "zl", "core"))
    rows = P(("blk", "zl", "core"), None)
    return jax.shard_map(
        body, mesh=fine, in_specs=(rows, rows, P(), P()), out_specs=(rows, rows), check_vma=False
    )
```
